256 devices in a mesh: dp: 8 (over z_hi, core), expert: 32 (over z_lo, y, x).
Axes of the slice: x: 4, y: 4, z: 8 (z_hi: 4, z_lo: 2; z = z_hi * 2 + z_lo), core: 2. Of those that a mesh axis runs over, the one named last changes fastest.
Arguments:
- out_cot: bfloat16 [32768, 4096], P(('dp', 'expert')), may hold values from -0.75 to 0.75
- route_ids: int32 [32768, 8], P(('dp', 'expert')), may hold values from 0 to 127, all different within a row; in each aligned block of 128 rows (0 to 127, 128 to 255, ...) at most 16 rows name the same one
- route_weight: float32 [32768, 8], P(('dp', 'expert')), may hold values from 0.05 to 0.4
- saved_gate: bfloat16 [8, 32, 512, 768], P('dp', 'expert'), may hold values from -6 to 6
- saved_up: bfloat16 [8, 32, 512, 768], P('dp', 'expert'), may hold values from -6 to 6
- down_weight: bfloat16 [32, 768, 4096], P('expert'), may hold values from -0.21875 to 0.21875
- moe_input: bfloat16 [32768, 4096], P(('dp', 'expert')), may hold values from -24 to 24
Outputs:
- gate_grad: bfloat16 [8, 32, 512, 768], P('dp', 'expert')
- up_grad: bfloat16 [8, 32, 512, 768], P('dp', 'expert')
- down_grad: float32 [32, 768, 4096], P('expert', 'dp')
- route_grad: float32 [32768, 8], P(('dp', 'expert'))
- router_grad: float32 [4096, 128], P(('dp', 'expert'))
The draws below stay inside these ranges and needn't reach their ends.
Inputs may be any that keep to these rules, and one draw needn't show every extreme that they name: `route_ids`: each row names 8 different experts; among the rows of one device (aligned blocks of 128 rows) no expert is named by more than 16 rows, a bound that some block reaches.
All inputs are finite; a program needn't handle non-finite values.
Results may differ from the reference program's by a relative error of at most 0.015.
Values may be sent and summed in bfloat16 or wider, within the bound.
A program may use at most 128 MiB of HBM per device.

```python
import math
import jax
import jax.numpy as jnp
import numpy as np
from jax import lax

D = 4096
TOPK = 8
FFE = 768
EXP_DEV = 4
TOK_DEV = 128
EXPERTS = 128
MOST = 16
SLOTS = 512
TOKENS = 32768
N_DP = 8
N_EXPERT = 32


def raised(values, own_key, source, target, parts, factor):
    owner, partner = [(jnp.arange(values.shape[dim]) // (values.shape[dim] // parts)).reshape([-1 if axis == dim else 1 for axis in range(values.ndim)]) for dim in (source, target)]
    chosen = jax.random.permutation(own_key, parts)[partner]
    strong = (owner == chosen) | (owner == (partner + parts // 2) % parts)
    return jnp.where(strong, factor * values, values)


def levels(stream_key, dims, shards, least, largest):
    def one(dim, parts):
        draws = jax.random.uniform(jax.random.fold_in(jax.random.fold_in(stream_key, 6), dim), (parts,), jnp.float32, least / len(shards), largest / len(shards))
        return jnp.repeat(jnp.exp(draws), dims[dim] // parts).reshape((-1,) + (1,) * (len(dims) - dim - 1))

    level = one(*shards[0])
    for cut in shards[1:]:
        level = level * one(*cut)
    return level


def routed_block(key, own, number, rows, number_of, top, bound, slope):
    ranking = jax.random.permutation(key, number_of)
    packed, ordinary = load_shares(number_of, rows * top, bound, slope, True), load_shares(number_of, rows * top, bound, slope, False)
    places = jnp.arange(number_of)

    def named(sizes, offset_by):
        used = int((sizes > 0).sum())
        fixed = max(1, used // 4)
        passed = fixed + (places - fixed + offset_by * (used - fixed)) % max(1, number_of - fixed)
        return jnp.zeros((number_of,), jnp.int32).at[ranking[jnp.where(places < fixed, places, passed)]].set(jnp.asarray(sizes, jnp.int32))

    sizes = jnp.where(number % 4 == 0, named(packed, number // 4), named(ordinary, number - number // 4 - 1))
    mixed = jax.random.permutation(jax.random.fold_in(own, 3), number_of)
    donor, sink = mixed[0:number_of // 2 * 2:2], mixed[1:number_of // 2 * 2:2]
    room = jnp.minimum(sizes[donor] - 1, bound - sizes[sink]) // 2
    room = jnp.where((donor == ranking[0]) | (sink == ranking[0]) | (sizes[sink] == 0), 0, jnp.maximum(room, 0))
    passed = jax.random.randint(jax.random.fold_in(own, 4), (number_of // 2,), 0, 1 << 20) % (room + 1)
    sizes = sizes.at[donor].add(-passed).at[sink].add(passed)
    members = jnp.searchsorted(jnp.cumsum(sizes), jnp.arange(rows * top), side="right").astype(jnp.int32)
    table = members.reshape(top, rows).T
    table = table[jax.random.permutation(jax.random.fold_in(own, 1), rows)]
    offset_by = jax.random.randint(jax.random.fold_in(own, 2), (rows, 1), 0, top)
    return jnp.take_along_axis(table, (jnp.arange(top)[None, :] + offset_by) % top, axis=1)


def load_shares(count, total, most, slope, full):
    loads = [(1 << 20) // math.isqrt(grade ** slope) + 1 for grade in range(1, count + 1)]
    largest = most if full else min(most, max(-(-total // count), total * loads[0] // sum(loads)))
    least = 1 if total - largest >= count - 1 else 0
    counts, rest = [largest] + [least] * (count - 1), total - largest - least * (count - 1)
    while rest > 0:
        free = [i for i in range(1, count) if counts[i] < largest] or [i for i in range(1, count) if counts[i] < most]
        pool, left = sum([loads[i] for i in free]), rest
        for i in free:
            extra = min(most - counts[i], max(1, left * loads[i] // pool), rest)
            counts[i] = counts[i] + extra
            rest = rest - extra
    return np.array(counts)


def gaussian(own_key, shape, deviation, reach, split=(), kind=jnp.bfloat16):
    values = jax.random.normal(own_key, shape, jnp.float32) * deviation
    if len(split) > 0:
        values = levels(own_key, shape, split, -0.22, 0.18) * values
    return jnp.clip(values, min=-reach, max=reach).astype(kind)


def gaussian_with(rng, extent, width, bound, pieces, heavy, held_as=jnp.bfloat16):
    values = width * jax.random.normal(rng, extent, jnp.float32)
    if pieces:
        values = values * levels(rng, extent, pieces, -0.22, 0.18)
    return jnp.clip(raised(values, jax.random.fold_in(rng, 3), *heavy), -bound, bound).astype(held_as)


def setup_inputs(seed: int = 0) -> dict:
    key_of = jax.random.split(jax.random.key(seed), 8)
    out_cot = gaussian(key_of[0], (TOKENS, D), 0.125, 0.75, ((0, 256),))
    route_ids_keys = jax.random.split(jax.random.fold_in(key_of[1], 1), TOKENS // TOK_DEV)
    route_ids_turns = jax.random.permutation(jax.random.fold_in(key_of[1], 3), TOKENS // TOK_DEV)
    route_ids = jax.vmap(lambda own, number: routed_block(jax.random.fold_in(key_of[1], 2), own, number, TOK_DEV, EXPERTS, TOPK, MOST, 2))(route_ids_keys, route_ids_turns).reshape((TOKENS, TOPK))
    route_weight = jnp.clip(0.05 + 0.35 * jax.random.uniform(key_of[2], (TOKENS, TOPK), jnp.float32) ** levels(key_of[2], (TOKENS, TOPK), ((0, 256),), -0.2, 0.2), 0.05, 0.4)
    saved_gate = gaussian(key_of[3], (N_DP, N_EXPERT, SLOTS, FFE), 1.0, 6.0, ((0, 8), (1, 32)))
    saved_up = gaussian(key_of[4], (N_DP, N_EXPERT, SLOTS, FFE), 1.0, 6.0, ((0, 8), (1, 32)))
    down_weight = gaussian(key_of[5], (N_EXPERT, FFE, D), FFE ** -0.5, 0.21875, ((0, 32),))
    moe_input = gaussian_with(key_of[6], (TOKENS, D), 1.0, 24.0, ((0, 256),), (0, 1, 256, 6.0))
    return dict(out_cot=out_cot, route_ids=route_ids, route_weight=route_weight, saved_gate=saved_gate, saved_up=saved_up, down_weight=down_weight, moe_input=moe_input)


def reference(out_cot, route_ids, route_weight, saved_gate, saved_up, down_weight, moe_input):
    group = N_EXPERT * TOK_DEV
    slots = N_EXPERT * MOST
    cot_groups = out_cot.reshape(N_DP, group, D)
    id_groups = route_ids.reshape(N_DP, group, TOPK)
    weight_groups = route_weight.reshape(N_DP, group, TOPK)

    def one_expert(carry, index):
        matrix = down_weight[index]

        def one_group(dpos):
            ids = id_groups[dpos]
            hit = ids == index * EXP_DEV
            hit_tok = jnp.sum(hit.astype(jnp.int32), -1)
            token_weight = jnp.sum(jnp.where(hit, weight_groups[dpos], 0.0), -1).astype(jnp.bfloat16)
            per_source = hit_tok.reshape(N_EXPERT, TOK_DEV)
            rank = jnp.cumsum(per_source, 1) - per_source
            source = jnp.arange(N_EXPERT, dtype=jnp.int32)[:, None]
            slot = jnp.where(per_source > 0, source * MOST + rank, slots).reshape(-1).astype(jnp.int32)
            rows = jnp.zeros((slots, D), jnp.bfloat16).at[slot].set(cot_groups[dpos], mode="drop")
            slot_weight = jnp.zeros((slots,), jnp.bfloat16).at[slot].set(token_weight, mode="drop")
            gate = saved_gate[dpos, index].astype(jnp.float32)
            upper = saved_up[dpos, index].astype(jnp.float32)
            sigma = jax.nn.sigmoid(gate)
            active = gate * sigma
            hidden = (active * upper).astype(jnp.bfloat16)
            expert_out = jnp.dot(hidden, matrix, preferred_element_type=jnp.float32)
            slot_dot = jnp.sum(expert_out * rows.astype(jnp.float32), -1)
            weighted = (slot_weight.astype(jnp.float32)[:, None] * rows.astype(jnp.float32)).astype(jnp.bfloat16)
            hidden_cot = lax.dot_general(weighted, matrix, (((1,), (1,)), ((), ())), preferred_element_type=jnp.float32)
            up_grad = (hidden_cot * active).astype(jnp.bfloat16)
            gate_grad = (hidden_cot * upper * sigma * (1.0 + gate * (1.0 - sigma))).astype(jnp.bfloat16)
            term = lax.dot_general(hidden, weighted, (((0,), (0,)), ((), ())), preferred_element_type=jnp.float32)
            term = lax.optimization_barrier(term.astype(jnp.bfloat16)).astype(jnp.float32)
            safe = jnp.minimum(slot, slots - 1)
            token_dot = jnp.where(hit_tok > 0, slot_dot[safe], 0.0)
            route = jnp.where(hit, token_dot[:, None], 0.0)
            return gate_grad, up_grad, term, route

        gate_grad, up_grad, terms, routes = lax.map(one_group, jnp.arange(N_DP, dtype=jnp.int32))
        return carry + routes, (gate_grad, up_grad, jnp.sum(terms, 0))

    start = jnp.zeros((N_DP, group, TOPK), jnp.float32)
    routes, (gate_all, up_all, down_grad) = lax.scan(one_expert, start, jnp.arange(N_EXPERT, dtype=jnp.int32))
    gate_grad = jnp.transpose(gate_all, (1, 0, 2, 3))
    up_grad = jnp.transpose(up_all, (1, 0, 2, 3))
    route_grad = routes.reshape(TOKENS, TOPK)
    mixed = jnp.sum(route_weight * route_grad, -1, keepdims=True)
    per_pick = route_weight * (route_grad - mixed)
    columns = jnp.arange(EXPERTS, dtype=jnp.int32)
    logit_cot = jnp.zeros((TOKENS, EXPERTS), jnp.float32)
    for pick in range(TOPK):
        logit_cot = logit_cot + jnp.where(route_ids[:, pick][:, None] == columns[None, :], per_pick[:, pick][:, None], 0.0)
    logit_cot = logit_cot.astype(jnp.bfloat16)
    router_grad = 0.015625 * jnp.dot(moe_input.T, logit_cot, preferred_element_type=jnp.float32)
    return gate_grad, up_grad, down_grad, route_grad, router_grad
```

```python
import jax
import jax.numpy as jnp
from jax import lax
from jax.sharding import PartitionSpec as P

EXP_DEV = 4


def per_device(out_cot, route_ids, route_weight, saved_gate, saved_up, down_weight, moe_input):
    n_expert = lax.axis_size("expert")
    slots = saved_gate.shape[2]
    most = slots // n_expert
    width = out_cot.shape[1]
    all_experts = EXP_DEV * n_expert
    hit = route_ids % EXP_DEV == 0
    target = route_ids // EXP_DEV
    targets = jnp.arange(n_expert, dtype=jnp.int32)
    select = hit[:, :, None] & (target[:, :, None] == targets[None, None, :])
    onehot = jnp.sum(select.astype(jnp.int32), 1)
    rank = jnp.cumsum(onehot, 0) - onehot
    places = jnp.arange(most, dtype=jnp.int32)
    placer = (onehot.T[:, None, :] == 1) & (rank.T[:, None, :] == places[None, :, None])
    placer_bf = placer.astype(jnp.bfloat16)
    placer_fl = placer.astype(jnp.float32)
    send_rows = jnp.einsum(
        "jrt,td->jrd", placer_bf, out_cot, preferred_element_type=jnp.float32
    ).astype(jnp.bfloat16)
    token_weight = jnp.sum(jnp.where(select, route_weight[:, :, None], 0.0), 1)
    send_weight = jnp.einsum(
        "jrt,tj->jr", placer_fl, token_weight, precision=lax.Precision.HIGHEST
    ).astype(jnp.bfloat16)
    recv_rows, recv_weight = (
        lax.all_to_all(send_rows, "expert", split_axis=0, concat_axis=0, tiled=True),
        lax.all_to_all(send_weight, "expert", split_axis=0, concat_axis=0, tiled=True),
    )
    rows = recv_rows.reshape(slots, width)
    slot_weight = recv_weight.reshape(slots)
    matrix = down_weight[0]
    gate = saved_gate[0, 0].astype(jnp.float32)
    upper = saved_up[0, 0].astype(jnp.float32)
    sigma = jax.nn.sigmoid(gate)
    active = gate * sigma
    hidden = (active * upper).astype(jnp.bfloat16)
    expert_out = jnp.dot(hidden, matrix, preferred_element_type=jnp.float32)
    slot_dot = jnp.sum(expert_out * rows.astype(jnp.float32), -1)
    back = lax.all_to_all(
        slot_dot.reshape(n_expert, most), "expert", split_axis=0, concat_axis=0, tiled=True
    )
    weighted = (slot_weight.astype(jnp.float32)[:, None] * rows.astype(jnp.float32)).astype(
        jnp.bfloat16
    )
    hidden_cot = lax.dot_general(
        weighted, matrix, (((1,), (1,)), ((), ())), preferred_element_type=jnp.float32
    )
    up_grad = (hidden_cot * active).astype(jnp.bfloat16)
    gate_grad = (hidden_cot * upper * sigma * (1.0 + gate * (1.0 - sigma))).astype(jnp.bfloat16)
    piece = hidden
    down_part = lax.psum_scatter(
        lax.dot_general(
            piece, weighted, (((0,), (0,)), ((), ())), preferred_element_type=jnp.float32
        ).astype(jnp.bfloat16),
        "dp",
        scatter_dimension=0,
        tiled=True,
    ).astype(jnp.float32)
    token_dot = jnp.einsum("jrt,jr->tj", placer_fl, back, precision=lax.Precision.HIGHEST)
    route_grad = jnp.sum(jnp.where(select, token_dot[:, None, :], 0.0), -1)
    mixed = jnp.sum(route_weight * route_grad, -1, keepdims=True)
    per_pick = route_weight * (route_grad - mixed)
    columns = jnp.arange(all_experts, dtype=jnp.int32)
    matches = route_ids[:, :, None] == columns[None, None, :]
    logit_cot = jnp.sum(jnp.where(matches, per_pick[:, :, None], 0.0), 1).astype(jnp.bfloat16)
    piece = moe_input
    product = lax.dot_general(
        piece, logit_cot, (((0,), (0,)), ((), ())), preferred_element_type=jnp.float32
    )
    n_dp = lax.axis_size("dp")
    own = product.shape[0] // (n_dp * n_expert)
    blocks = (0.015625 * product).reshape(n_dp, n_expert, own, all_experts)
    across = lax.all_to_all(blocks, "expert", split_axis=1, concat_axis=1, tiled=True)
    partial = jnp.sum(across, 1)
    along = lax.all_to_all(partial, "dp", split_axis=0, concat_axis=0, tiled=True)
    router_part = jnp.sum(along, 0)
    return (gate_grad[None, None], up_grad[None, None], down_part[None], route_grad, router_part)


def solution(mesh):
    placed = (
        P(("dp", "expert"), None),
        P(("dp", "expert"), None),
        P(("dp", "expert"), None),
        P("dp", "expert", None, None),
        P("dp", "expert", None, None),
        P("expert", None, None),
        P(("dp", "expert"), None),
    )
    return jax.shard_map(
        per_device,
        mesh=mesh,
        in_specs=placed,
        out_specs=(
            P("dp", "expert", None, None),
            P("dp", "expert", None, None),
            P("expert", "dp", None),
            P(("dp", "expert"), None),
            P(("dp", "expert"), None),
        ),
        check_vma=False,
    )
```

```python
import functools

import jax
import jax.numpy as jnp
from jax import lax
from jax.experimental import pallas as pl
from jax.experimental.pallas import tpu as pltpu
from jax.sharding import PartitionSpec as P

EXP_DEV = 4
TOK = 128
TOPK = 8
D = 4096
FFE = 768
SLOTS = 512
HALF = SLOTS // 2
EXPERTS = 128
MOST = 16
NC = 4
DC = D // NC
DH = DC // 2
OWN = FFE // 8
MESH = pl.DeviceIdType.MESH
F32 = jnp.float32
BF = jnp.bfloat16


def dot(a, b, ca=1, cb=0):
    return lax.dot_general(a, b, (((ca,), (cb,)), ((), ())), preferred_element_type=F32)


def m16(index):
    return pl.multiple_of(index * 16, 16)


def body(
    tok, ids, rw, gate_hbm, up_hbm, w_hbm, moe_hbm,
    gate_out, up_out, down_out, route_out, router_out,
    gate, up, w, moe, moe_t, placer, placer_t, placer_p, tok_p, weight_by_expert,
    w_send, w_recv, snd, recv, hidden, active, gate_factor, hw_t, hc,
    term, pair, psum, ring, back_send, back_recv,
    prod, prod_b, rp, rq_send, rq, rz_send, rz, gate_v, up_v, down_v,
    in_sem, z_s, z_r, w_s, w_r, a_s, a_r, p_s, p_r, g_s, g_r, b_s, b_r,
    rp_s, rp_r, rq_s, rq_r, rz_s, rz_r, out_sem,
):
    d = lax.axis_index("dp")
    e = lax.axis_index("expert")
    zhi, core = d // 2, d % 2
    zlo, yx = e // 16, e % 16
    y, x = yx // 4, yx % 4
    sibling = (zhi * 2 + 1 - core, e)
    partner = (d, (1 - zlo) * 16 + yx)
    up_ring = (((zhi + 1) % 4) * 2 + core, e)
    down_ring = (((zhi + 3) % 4) * 2 + core, e)
    z = zhi * 2 + zlo

    def column(k):
        other = (z + k) % 8
        return other, ((other // 2) * 2 + core, (other % 2) * 16 + yx)

    def plane(k):
        step = (k * 5) % 16
        return ((y + step // 4) % 4) * 4 + (x + step % 4) % 4

    def send(src, dst, s, r, target):
        pltpu.make_async_remote_copy(src, dst, s, r, target, MESH).start()

    def drain(ref, sem):
        pltpu.make_async_copy(ref, ref, sem).wait()

    bar = pltpu.get_barrier_semaphore()

    def greet(k, carry):
        pl.semaphore_signal(bar, inc=1, device_id=(d, (e + k) % 32), device_id_type=MESH)
        return carry

    lax.fori_loop(1, 32, greet, 0)
    pl.semaphore_signal(bar, inc=1, device_id=sibling, device_id_type=MESH)

    def greet_column(k, carry):
        pl.semaphore_signal(
            bar, inc=1, device_id=(((zhi + k) % 4) * 2 + core, e), device_id_type=MESH
        )
        pl.semaphore_signal(
            bar, inc=1, device_id=(((zhi + k) % 4) * 2 + core, (1 - zlo) * 16 + yx), device_id_type=MESH
        )
        return carry

    lax.fori_loop(1, 4, greet_column, 0)

    loads = [
        pltpu.make_async_copy(gate_hbm, gate, in_sem.at[0]),
        pltpu.make_async_copy(up_hbm, up, in_sem.at[1]),
        pltpu.make_async_copy(moe_hbm, moe, in_sem.at[2]),
        pltpu.make_async_copy(w_hbm, w, in_sem.at[3]),
    ]
    for load in loads:
        load.start()

    lane = lax.broadcasted_iota(jnp.int32, (TOK, EXPERTS), 1)
    row = lax.broadcasted_iota(jnp.int32, (TOK, EXPERTS), 0)
    named = jnp.zeros((TOK, EXPERTS), F32)
    weights = jnp.zeros((TOK, EXPERTS), F32)
    for k in range(TOPK):
        match = ids[:, k : k + 1] == lane
        named = named + jnp.where(match, 1.0, 0.0)
        weights = weights + jnp.where(match, rw[:, k : k + 1], 0.0)
    weight_by_expert[...] = weights
    before = jnp.where(lane < row, 1.0, 0.0).astype(BF)
    rank = dot(before, named.astype(BF))
    code = (named * (rank + 1.0)).astype(BF)
    slot_row = lax.broadcasted_iota(jnp.int32, (SLOTS, EXPERTS), 0)
    slot_lane = lax.broadcasted_iota(jnp.int32, (SLOTS, EXPERTS), 1)
    chooser = jnp.where(slot_lane == EXP_DEV * (slot_row // MOST), 1.0, 0.0)
    chooser_b = chooser.astype(BF)
    placed = dot(chooser_b, code, 1, 1) == (slot_row % MOST + 1).astype(F32)
    placer[...] = jnp.where(placed, 1.0, 0.0).astype(BF)
    slot_weights = jnp.sum(jnp.where(placed, dot(chooser_b, weights.astype(BF), 1, 1), 0.0), 1, keepdims=True)
    w_send[...] = jnp.broadcast_to(slot_weights, (SLOTS, 128)).astype(BF)
    t_row = lax.broadcasted_iota(jnp.int32, (EXPERTS, SLOTS), 0)
    t_col = lax.broadcasted_iota(jnp.int32, (EXPERTS, SLOTS), 1)
    chooser_t = jnp.where(t_row == EXP_DEV * (t_col // MOST), 1.0, 0.0).astype(BF)
    placed_t = dot(code, chooser_t) == (
        lax.broadcasted_iota(jnp.int32, (TOK, SLOTS), 1) % MOST + 1
    ).astype(F32)
    placer_t[...] = jnp.where(placed_t, 1.0, 0.0).astype(BF)

    pl.semaphore_wait(bar, 38)

    send(placer.at[pl.ds(pl.multiple_of((1 - zlo) * HALF, HALF), HALF)], placer_p, z_s, z_r.at[NC], partner)
    for c in range(NC):
        cols = pl.ds(c * DC, DC)
        send(tok.at[:, cols], tok_p.at[:, cols], z_s, z_r.at[c], partner)

    def pack(half, c):
        cols = pl.ds(c * DC, DC)
        if half == 0:
            chosen = placer[pl.ds(pl.multiple_of(zlo * HALF, HALF), HALF), :]
            tokens = tok
        else:
            chosen = placer_p[...]
            tokens = tok_p
        for q in range(DC // 256):
            part = pl.ds(c * DC + q * 256, 256)
            snd[pl.ds(half * HALF, HALF), part] = dot(chosen, tokens[:, part]).astype(BF)
        source = zlo * 16 + yx if half == 0 else (1 - zlo) * 16 + yx
        recv[pl.ds(m16(source), 16), cols] = snd[pl.ds(m16(half * 16 + yx), 16), cols]

        def one(k, carry):
            target = plane(k)
            send(
                snd.at[pl.ds(m16(half * 16 + target), 16), cols],
                recv.at[pl.ds(m16(source), 16), cols],
                a_s, a_r.at[c, half], (d, zlo * 16 + target),
            )
            return carry

        lax.fori_loop(1, 16, one, 0)

    def pack_partner(c):
        drain(tok_p.at[:, pl.ds(c * DC, DC)], z_r.at[c])
        pack(1, c)

    pack(0, 0)

    w_recv[pl.ds(m16(e), 16), :] = w_send[pl.ds(m16(e), 16), :]

    def give_weight(k, carry):
        target = (e + k) % 32
        send(w_send.at[pl.ds(m16(target), 16)], w_recv.at[pl.ds(m16(e), 16)], w_s, w_r, (d, target))
        return carry

    lax.fori_loop(1, 32, give_weight, 0)

    pack(0, 1)

    loads[0].wait()
    loads[1].wait()

    def gates(i, carry):
        part = pl.ds(pl.multiple_of(i * 32, 32), 32)
        g = gate[part, :].astype(F32)
        u = up[part, :].astype(F32)
        sigma = jax.nn.sigmoid(g)
        act = g * sigma
        active[part, :] = act
        gate_factor[part, :] = u * sigma * (1.0 + g * (1.0 - sigma))
        hidden[part, :] = (act * u).astype(BF)
        return carry

    lax.fori_loop(0, SLOTS // 32, gates, 0)

    drain(placer_p, z_r.at[NC])
    pack_partner(0)
    pack(0, 2)

    loads[2].wait()

    def turn(i, carry):
        part = pl.ds(pl.multiple_of(i * 512, 512), 512)
        moe_t[part, :] = moe[:, part].T
        return carry

    lax.fori_loop(0, D // 512, turn, 0)

    drain(w_recv.at[pl.ds(0, SLOTS - 16)], w_r)

    def weigh(i, carry):
        part = pl.ds(pl.multiple_of(i * 128, 128), 128)
        scale = jnp.concatenate([w_recv[part, :].astype(F32)] * (FFE // 128), axis=1)
        hw_t[:, part] = (scale * hidden[part, :].astype(F32)).astype(BF).T
        return carry

    lax.fori_loop(0, SLOTS // 128, weigh, 0)

    pack_partner(1)
    pack(0, 3)
    loads[3].wait()

    def arrive(c):
        for half in range(2):
            drain(recv.at[pl.ds(0, HALF - 16), pl.ds(c * DC, DC)], a_r.at[c, half])

    def make_term(c):
        def one(q, carry):
            inner = pl.ds(pl.multiple_of(q * 256, 256), 256)
            outer = pl.ds(pl.multiple_of(c * DC + q * 256, 256), 256)
            block = dot(hw_t[...], recv[:, outer]).astype(BF)
            term[c, :, :, inner] = block.reshape(8, OWN, 256)
            return carry

        lax.fori_loop(0, DC // 256, one, 0)

        def give(k, carry):
            send(term.at[c, 2 * k + 1 - core], pair.at[c, k], p_s, p_r.at[c], sibling)
            return carry

        lax.fori_loop(0, 4, give, 0)

    def make_hidden(c):
        cols = pl.ds(c * DC, DC)

        def one(q, carry):
            part = pl.ds(pl.multiple_of(q * 256, 256), 256)
            block = dot(recv[:, cols], w[part, cols], 1, 1)
            if c == 0:
                hc[:, part] = block
            else:
                hc[:, part] = hc[:, part] + block
            return carry

        lax.fori_loop(0, FFE // 256, one, 0)

    left, right = pl.ds(0, DH), pl.ds(DH, DH)

    def ring_send(c, step, first, second):
        send(first, ring.at[c, step, 0], g_s, g_r.at[c, step, 0], up_ring)
        send(second, ring.at[c, step, 1], g_s, g_r.at[c, step, 1], down_ring)

    def pair_sum(c):
        drain(pair.at[c], p_r.at[c])

        def one(k, carry):
            psum[c, k] = (term[c, 2 * k + core].astype(F32) + pair[c, k].astype(F32)).astype(BF)
            return carry

        lax.fori_loop(0, 4, one, 0)
        ring_send(
            c, 0, psum.at[c, (zhi + 3) % 4, :, left], psum.at[c, (zhi + 1) % 4, :, right]
        )

    def ring_step(c, step):
        for way, half, index in ((0, left, (zhi + 6 - step) % 4), (1, right, (zhi + 2 + step) % 4)):
            drain(ring.at[c, step, way], g_r.at[c, step, way])
            total = ring[c, step, way].astype(F32) + psum[c, index, :, half].astype(F32)
            ring[c, step, way] = total.astype(BF)
        ring_send(c, step + 1, ring.at[c, step, 0], ring.at[c, step, 1])

    outs = [
        pltpu.make_async_copy(gate_v, gate_out, out_sem.at[0]),
        pltpu.make_async_copy(up_v, up_out, out_sem.at[1]),
    ]
    down_outs = [
        pltpu.make_async_copy(
            down_v.at[:, pl.ds(c * DC, DC)], down_out.at[:, pl.ds(c * DC, DC)], out_sem.at[2 + c]
        )
        for c in range(NC)
    ]

    def ring_end(c):
        for way, half in ((0, left), (1, right)):
            drain(ring.at[c, 2, way], g_r.at[c, 2, way])
            total = ring[c, 2, way].astype(F32) + psum[c, zhi, :, half].astype(F32)
            down_v[:, pl.ds(c * DC + way * DH, DH)] = total
        down_outs[c].start()

    def progress(c, stage):
        if stage == 0:
            pair_sum(c)
        elif stage < 3:
            ring_step(c, stage - 1)
        else:
            ring_end(c)

    arrive(0)
    make_term(0)
    pack_partner(2)
    make_hidden(0)
    progress(0, 0)
    pack_partner(3)

    arrive(1)
    make_term(1)
    progress(0, 1)
    make_hidden(1)
    progress(1, 0)
    progress(0, 2)

    arrive(2)
    make_term(2)
    progress(1, 1)
    make_hidden(2)
    progress(2, 0)
    progress(0, 3)
    progress(1, 2)

    arrive(3)
    make_term(3)
    progress(2, 1)
    make_hidden(3)

    def dots(i, carry):
        part = pl.ds(pl.multiple_of(i * 32, 32), 32)
        value = jnp.sum(hidden[part, :].astype(F32) * hc[part, :], 1, keepdims=True)
        back_send[part, :] = jnp.broadcast_to(value, (32, 128))
        return carry

    lax.fori_loop(0, SLOTS // 32, dots, 0)
    back_recv[pl.ds(m16(e), 16), :] = back_send[pl.ds(m16(e), 16), :]

    def give_back(k, carry):
        target = (e + k) % 32
        send(back_send.at[pl.ds(m16(target), 16)], back_recv.at[pl.ds(m16(e), 16)], b_s, b_r, (d, target))
        return carry

    lax.fori_loop(1, 32, give_back, 0)
    progress(3, 0)

    def grads(i, carry):
        part = pl.ds(pl.multiple_of(i * 32, 32), 32)
        scale = jnp.concatenate([w_recv[part, :].astype(F32)] * (FFE // 128), axis=1)
        cot = hc[part, :] * scale
        up_v[part, :] = (cot * active[part, :]).astype(BF)
        gate_v[part, :] = (cot * gate_factor[part, :]).astype(BF)
        return carry

    lax.fori_loop(0, SLOTS // 32, grads, 0)
    outs[0].start()
    outs[1].start()
    progress(1, 3)

    drain(back_recv.at[pl.ds(0, SLOTS - 16)], b_r)
    spread = back_recv[...] * chooser
    high = spread.astype(BF)
    rest = spread - high.astype(F32)
    middle = rest.astype(BF)
    low = (rest - middle.astype(F32)).astype(BF)
    by_expert = dot(placer_t[...], high) + dot(placer_t[...], middle) + dot(placer_t[...], low)
    column8 = lax.broadcasted_iota(jnp.int32, (TOK, TOPK), 1)
    routes = jnp.zeros((TOK, TOPK), F32)
    for k in range(TOPK):
        found = jnp.sum(jnp.where(ids[:, k : k + 1] == lane, by_expert, 0.0), 1, keepdims=True)
        routes = jnp.where(column8 == k, found, routes)
    route_out[...] = routes
    mine = weight_by_expert[...]
    mixed = jnp.sum(mine * by_expert, 1, keepdims=True)
    logit = (mine * (by_expert - mixed)).astype(BF)

    def product(i, carry):
        block = dot(moe_t[pl.ds(pl.multiple_of(i * 512, 512), 512), :], logit)
        prod[i] = block
        prod_b[i] = block.astype(BF)
        return carry

    lax.fori_loop(0, 8, product, 0)

    def give_pair(k, carry):
        send(prod_b.at[2 * k + 1 - core], rp.at[k], rp_s, rp_r, sibling)
        return carry

    lax.fori_loop(0, 4, give_pair, 0)
    progress(2, 2)
    progress(3, 1)

    drain(rp, rp_r)

    def pair_router(k, carry):
        both = prod[2 * k + core] + rp[k].astype(F32)
        rq_send[pl.ds(2 * k, 2)] = both.astype(BF).reshape(2, HALF, 128)
        return carry

    lax.fori_loop(0, 4, pair_router, 0)
    rq[yx] = rq_send[:, pl.ds(m16(yx), 16), :]

    def give_plane(k, carry):
        target = plane(k)
        send(rq_send.at[:, pl.ds(m16(target), 16)], rq.at[yx], rq_s, rq_r, (d, zlo * 16 + target))
        return carry

    lax.fori_loop(1, 16, give_plane, 0)
    progress(2, 3)
    drain(rq.at[pl.ds(0, 15)], rq_r)

    def add_plane(k, total):
        return total + rq[k].astype(F32)

    rz_send[...] = lax.fori_loop(1, 16, add_plane, rq[0].astype(F32)).astype(BF)
    rz[z] = rz_send[z]

    def give_column(k, carry):
        other, target = column(k)
        send(rz_send.at[other], rz.at[z], rz_s, rz_r, target)
        return carry

    lax.fori_loop(1, 8, give_column, 0)
    progress(3, 2)
    drain(rz.at[pl.ds(0, 7)], rz_r)
    total = rz[0].astype(F32)
    for k in range(1, 8):
        total = total + rz[k].astype(F32)
    router_out[...] = 0.015625 * total
    progress(3, 3)

    drain(placer_p, z_s)
    drain(tok_p, z_s)
    drain(w_recv.at[pl.ds(0, SLOTS - 16)], w_s)
    drain(recv.at[pl.ds(0, SLOTS - 32)], a_s)
    drain(pair, p_s)
    drain(ring, g_s)
    drain(back_recv.at[pl.ds(0, SLOTS - 16)], b_s)
    drain(rp, rp_s)
    drain(rq.at[pl.ds(0, 15)], rq_s)
    drain(rz.at[pl.ds(0, 7)], rz_s)
    outs[0].wait()
    outs[1].wait()
    for copy in down_outs:
        copy.wait()


def per_device(out_cot, route_ids, route_weight, saved_gate, saved_up, down_weight, moe_input):
    vmem = pl.BlockSpec(memory_space=pltpu.VMEM)
    anywhere = pl.BlockSpec(memory_space=pl.ANY)
    dma = pltpu.SemaphoreType.DMA
    scratch = [
        ((SLOTS, FFE), BF),
        ((SLOTS, FFE), BF),
        ((FFE, D), BF),
        ((TOK, D), BF),
        ((D, TOK), BF),
        ((SLOTS, TOK), BF),
        ((TOK, SLOTS), BF),
        ((HALF, TOK), BF),
        ((TOK, D), BF),
        ((TOK, EXPERTS), F32),
        ((SLOTS, 128), BF),
        ((SLOTS, 128), BF),
        ((SLOTS, D), BF),
        ((SLOTS, D), BF),
        ((SLOTS, FFE), BF),
        ((SLOTS, FFE), F32),
        ((SLOTS, FFE), F32),
        ((FFE, SLOTS), BF),
        ((SLOTS, FFE), F32),
        ((NC, 8, OWN, DC), BF),
        ((NC, 4, OWN, DC), BF),
        ((NC, 4, OWN, DC), BF),
        ((NC, 3, 2, OWN, DH), BF),
        ((SLOTS, 128), F32),
        ((SLOTS, 128), F32),
        ((8, 512, 128), F32),
        ((8, 512, 128), BF),
        ((4, 512, 128), BF),
        ((8, HALF, 128), BF),
        ((16, 8, 16, 128), BF),
        ((8, 16, 128), BF),
        ((8, 16, 128), BF),
        ((SLOTS, FFE), BF),
        ((SLOTS, FFE), BF),
        ((OWN, D), F32),
    ]
    sems = [
        dma((4,)), dma(()), dma((NC + 1,)), dma(()), dma(()), dma(()), dma((NC, 2)),
        dma(()), dma((NC,)), dma(()), dma((NC, 3, 2)), dma(()), dma(()),
        dma(()), dma(()), dma(()), dma(()), dma(()), dma(()), dma((2 + NC,)),
    ]
    outs = pl.pallas_call(
        body,
        out_shape=(
            jax.ShapeDtypeStruct((SLOTS, FFE), BF),
            jax.ShapeDtypeStruct((SLOTS, FFE), BF),
            jax.ShapeDtypeStruct((OWN, D), F32),
            jax.ShapeDtypeStruct((TOK, TOPK), F32),
            jax.ShapeDtypeStruct((16, EXPERTS), F32),
        ),
        in_specs=[vmem] * 3 + [anywhere] * 4,
        out_specs=(anywhere, anywhere, anywhere, vmem, vmem),
        scratch_shapes=[pltpu.VMEM(shape, kind) for shape, kind in scratch] + sems,
        compiler_params=pltpu.CompilerParams(
            collective_id=0, has_side_effects=True, vmem_limit_bytes=58 * 2**20
        ),
    )(out_cot, route_ids, route_weight, saved_gate[0, 0], saved_up[0, 0], down_weight[0], moe_input)
    gate_grad, up_grad, down_grad, route_grad, router_grad = outs
    return gate_grad[None, None], up_grad[None, None], down_grad[None], route_grad, router_grad


def solution(mesh):
    placed = (
        P(("dp", "expert"), None),
        P(("dp", "expert"), None),
        P(("dp", "expert"), None),
        P("dp", "expert", None, None),
        P("dp", "expert", None, None),
        P("expert", None, None),
        P(("dp", "expert"), None),
    )
    return jax.shard_map(
        per_device,
        mesh=mesh,
        in_specs=placed,
        out_specs=(
            P("dp", "expert", None, None),
            P("dp", "expert", None, None),
            P("expert", "dp", None),
            P(("dp", "expert"), None),
            P(("dp", "expert"), None),
        ),
        check_vma=False,
    )
```

```python
import functools

import jax
import jax.numpy as jnp
from jax import lax
from jax.experimental import pallas as pl
from jax.experimental.pallas import tpu as pltpu
from jax.sharding import PartitionSpec as P

EXP_DEV = 4
TOK = 128
TOPK = 8
D = 4096
FFE = 768
SLOTS = 512
HALF = SLOTS // 2
EXPERTS = 128
MOST = 16
NC = 8
DC = D // NC
DH = DC // 2
OWN = FFE // 8
MESH = pl.DeviceIdType.MESH
F32 = jnp.float32
BF = jnp.bfloat16


def dot(a, b, ca=1, cb=0):
    return lax.dot_general(a, b, (((ca,), (cb,)), ((), ())), preferred_element_type=F32)


def m16(index):
    return pl.multiple_of(index * 16, 16)


def body(
    tok_hbm, ids_hbm, rw_hbm, gate_hbm, up_hbm, w_hbm, moe_hbm,
    gate_out, up_out, down_out, route_out, router_out,
    tok, ids, rw, gate, up, w, moe, moe_t, placer, placer_p, tok_p, weight_by_expert,
    w_send, w_recv, snd, recv, hidden, active, gate_factor, hw_t, hc,
    term, pair, psum, ring, back_send, back_recv,
    prod, prod_b, rp, rq_send, rq, rz_send, rz, gate_v, up_v, down_v, route_v, router_v,
    in_sem, z_s, z_r, w_s, w_r, a_s, a_r, p_s, p_r, g_s, g_r, b_s, b_r,
    rp_s, rp_r, rq_s, rq_r, rz_s, rz_r, out_sem, logit,
):
    d = lax.axis_index("dp")
    e = lax.axis_index("expert")
    zhi, core = d // 2, d % 2
    zlo, yx = e // 16, e % 16
    y, x = yx // 4, yx % 4
    sibling = (zhi * 2 + 1 - core, e)
    partner = (d, (1 - zlo) * 16 + yx)
    up_ring = (((zhi + 1) % 4) * 2 + core, e)
    down_ring = (((zhi + 3) % 4) * 2 + core, e)
    z = zhi * 2 + zlo

    def column(k):
        other = (z + k) % 8
        return other, ((other // 2) * 2 + core, (other % 2) * 16 + yx)

    def plane(k):
        step = (k * 5) % 16
        return ((y + step // 4) % 4) * 4 + (x + step % 4) % 4

    def send(src, dst, s, r, target):
        pltpu.make_async_remote_copy(src, dst, s, r, target, MESH).start()

    def drain(ref, sem):
        pltpu.make_async_copy(ref, ref, sem).wait()

    bar = pltpu.get_barrier_semaphore()

    def greet(k, carry):
        pl.semaphore_signal(bar, inc=1, device_id=(d, (e + k) % 32), device_id_type=MESH)
        return carry

    lax.fori_loop(1, 32, greet, 0)
    pl.semaphore_signal(bar, inc=1, device_id=sibling, device_id_type=MESH)

    def greet_column(k, carry):
        pl.semaphore_signal(
            bar, inc=1, device_id=(((zhi + k) % 4) * 2 + core, e), device_id_type=MESH
        )
        pl.semaphore_signal(
            bar, inc=1, device_id=(((zhi + k) % 4) * 2 + core, (1 - zlo) * 16 + yx), device_id_type=MESH
        )
        return carry

    lax.fori_loop(1, 4, greet_column, 0)

    loads = [
        pltpu.make_async_copy(source, here, in_sem.at[i])
        for i, (source, here) in enumerate(
            (
                (ids_hbm, ids), (rw_hbm, rw), (tok_hbm, tok), (gate_hbm, gate),
                (up_hbm, up), (moe_hbm, moe), (w_hbm, w),
            )
        )
    ]
    for load in loads:
        load.start()
    load_ids, load_rw, load_tok, load_gate, load_up, load_moe, load_w = loads
    load_ids.wait()
    load_rw.wait()

    expert_row = lax.broadcasted_iota(jnp.int32, (EXPERTS, TOK), 0)
    token_lane = lax.broadcasted_iota(jnp.int32, (EXPERTS, TOK), 1)
    named = jnp.zeros((EXPERTS, TOK), F32)
    weights = jnp.zeros((EXPERTS, TOK), F32)
    for k in range(TOPK):
        match = ids[k : k + 1, :] == expert_row
        named = named + jnp.where(match, 1.0, 0.0)
        weights = weights + jnp.where(match, rw[k : k + 1, :], 0.0)
    weight_by_expert[...] = weights
    before = jnp.where(expert_row < token_lane, 1.0, 0.0).astype(BF)
    rank = dot(named.astype(BF), before)
    code = (named * (rank + 1.0)).astype(BF)
    slot_row = lax.broadcasted_iota(jnp.int32, (SLOTS, EXPERTS), 0)
    slot_lane = lax.broadcasted_iota(jnp.int32, (SLOTS, EXPERTS), 1)
    chooser = jnp.where(slot_lane == EXP_DEV * (slot_row // MOST), 1.0, 0.0)
    chooser_b = chooser.astype(BF)
    placed = dot(chooser_b, code) == (slot_row % MOST + 1).astype(F32)
    placer[...] = jnp.where(placed, 1.0, 0.0).astype(BF)
    slot_weights = jnp.sum(
        jnp.where(placed, dot(chooser_b, weights.astype(BF)), 0.0), 1, keepdims=True
    )
    w_send[...] = jnp.broadcast_to(slot_weights, (SLOTS, 128)).astype(BF)
    load_tok.wait()

    pl.semaphore_wait(bar, 38)

    w_recv[pl.ds(m16(e), 16), :] = w_send[pl.ds(m16(e), 16), :]

    def give_weight(k, carry):
        target = (e + k) % 32
        send(w_send.at[pl.ds(m16(target), 16)], w_recv.at[pl.ds(m16(e), 16)], w_s, w_r, (d, target))
        return carry

    lax.fori_loop(1, 32, give_weight, 0)

    send(placer.at[pl.ds(pl.multiple_of((1 - zlo) * HALF, HALF), HALF)], placer_p, z_s, z_r.at[NC], partner)
    for c in range(NC):
        cols = pl.ds(c * DC, DC)
        send(tok.at[:, cols], tok_p.at[:, cols], z_s, z_r.at[c], partner)

    def pack(half, c):
        cols = pl.ds(c * DC, DC)
        if half == 0:
            chosen = placer[pl.ds(pl.multiple_of(zlo * HALF, HALF), HALF), :]
            tokens = tok
        else:
            chosen = placer_p[...]
            tokens = tok_p
        for q in range(DC // 256):
            part = pl.ds(c * DC + q * 256, 256)
            snd[pl.ds(half * HALF, HALF), part] = dot(chosen, tokens[:, part]).astype(BF)
        source = zlo * 16 + yx if half == 0 else (1 - zlo) * 16 + yx
        recv[pl.ds(m16(source), 16), cols] = snd[pl.ds(m16(half * 16 + yx), 16), cols]

        def one(k, carry):
            target = plane(k)
            send(
                snd.at[pl.ds(m16(half * 16 + target), 16), cols],
                recv.at[pl.ds(m16(source), 16), cols],
                a_s, a_r.at[c, half], (d, zlo * 16 + target),
            )
            return carry

        lax.fori_loop(1, 16, one, 0)

    def pack_partner(c):
        if c == 0:
            drain(placer_p, z_r.at[NC])
        drain(tok_p.at[:, pl.ds(c * DC, DC)], z_r.at[c])
        pack(1, c)

    def gates(i, carry):
        part = pl.ds(pl.multiple_of(i * 32, 32), 32)
        g = gate[part, :].astype(F32)
        u = up[part, :].astype(F32)
        sigma = jax.nn.sigmoid(g)
        act = g * sigma
        active[part, :] = act
        gate_factor[part, :] = u * sigma * (1.0 + g * (1.0 - sigma))
        hidden[part, :] = (act * u).astype(BF)
        return carry

    def make_gates():
        load_gate.wait()
        load_up.wait()
        lax.fori_loop(0, SLOTS // 32, gates, 0)

    def turn(i, carry):
        part = pl.ds(pl.multiple_of(i * 512, 512), 512)
        moe_t[part, :] = moe[:, part].T
        return carry

    def turn_moe():
        load_moe.wait()
        lax.fori_loop(0, D // 512, turn, 0)

    def weigh(i, carry):
        part = pl.ds(pl.multiple_of(i * 128, 128), 128)
        scale = jnp.concatenate([w_recv[part, :].astype(F32)] * (FFE // 128), axis=1)
        hw_t[:, part] = (scale * hidden[part, :].astype(F32)).astype(BF).T
        return carry

    def weigh_hidden():
        drain(w_recv.at[pl.ds(0, SLOTS - 16)], w_r)
        lax.fori_loop(0, SLOTS // 128, weigh, 0)

    def arrive(c):
        for half in range(2):
            drain(recv.at[pl.ds(0, HALF - 16), pl.ds(c * DC, DC)], a_r.at[c, half])

    def make_term(c):
        arrive(c)
        for q in range(DC // 256):
            cols = pl.ds(c * DC + q * 256, 256)
            block = dot(hw_t[...], recv[:, cols]).astype(BF)
            term[:, :, :, cols] = block.reshape(4, 2, OWN, 256)
        cols = pl.ds(c * DC, DC)
        send(term.at[:, 1 - core, :, cols], pair.at[:, :, cols], p_s, p_r.at[c], sibling)

    def make_hidden(c):
        if c == 1:
            load_w.wait()
        cols = pl.ds((c - 1) * DC, 2 * DC)

        def one(q, carry):
            part = pl.ds(pl.multiple_of(q * 256, 256), 256)
            block = dot(recv[:, cols], w[part, cols], 1, 1)
            if c == 1:
                hc[:, part] = block
            else:
                hc[:, part] = hc[:, part] + block
            return carry

        lax.fori_loop(0, FFE // 256, one, 0)

    def ways(c):
        return (
            (0, pl.ds(c * DC, DH), up_ring, 1),
            (1, pl.ds(c * DC + DH, DH), down_ring, -1),
        )

    def pair_sum(c):
        cols = pl.ds(c * DC, DC)
        drain(pair.at[:, :, cols], p_r.at[c])

        def one(k, carry):
            both = term[k, core, :, cols].astype(F32) + pair[k, :, cols].astype(F32)
            psum[k, :, cols] = both.astype(BF)
            return carry

        lax.fori_loop(0, 4, one, 0)
        for way, part, target, sign in ways(c):
            block = (zhi + 4 - sign) % 4
            send(psum.at[block, :, part], ring.at[0, :, part], g_s, g_r.at[c, 0, way], target)

    def ring_step(c, step):
        for way, part, target, sign in ways(c):
            drain(ring.at[step, :, part], g_r.at[c, step, way])
            block = (zhi + 8 - sign * (step + 2)) % 4
            total = ring[step, :, part].astype(F32) + psum[block, :, part].astype(F32)
            ring[step, :, part] = total.astype(BF)
            send(ring.at[step, :, part], ring.at[step + 1, :, part], g_s, g_r.at[c, step + 1, way], target)

    outs = [
        pltpu.make_async_copy(gate_v, gate_out, out_sem.at[0]),
        pltpu.make_async_copy(up_v, up_out, out_sem.at[1]),
        pltpu.make_async_copy(route_v, route_out, out_sem.at[2]),
        pltpu.make_async_copy(router_v, router_out, out_sem.at[3]),
    ]
    down_outs = [
        pltpu.make_async_copy(
            down_v.at[:, pl.ds(c * DC, DC)], down_out.at[:, pl.ds(c * DC, DC)], out_sem.at[4 + c]
        )
        for c in range(NC)
    ]

    def ring_end(c):
        for way, part, target, sign in ways(c):
            drain(ring.at[2, :, part], g_r.at[c, 2, way])
            down_v[:, part] = ring[2, :, part].astype(F32) + psum[zhi, :, part].astype(F32)
        down_outs[c].start()

    def dots(i, carry):
        part = pl.ds(pl.multiple_of(i * 32, 32), 32)
        value = jnp.sum(hidden[part, :].astype(F32) * hc[part, :], 1, keepdims=True)
        back_send[part, :] = jnp.broadcast_to(value, (32, 128))
        return carry

    def give_back(k, carry):
        target = (e + k) % 32
        send(back_send.at[pl.ds(m16(target), 16)], back_recv.at[pl.ds(m16(e), 16)], b_s, b_r, (d, target))
        return carry

    def give_dots():
        lax.fori_loop(0, SLOTS // 32, dots, 0)
        back_recv[pl.ds(m16(e), 16), :] = back_send[pl.ds(m16(e), 16), :]
        lax.fori_loop(1, 32, give_back, 0)

    def grads(i, carry):
        part = pl.ds(pl.multiple_of(i * 32, 32), 32)
        scale = jnp.concatenate([w_recv[part, :].astype(F32)] * (FFE // 128), axis=1)
        cot = hc[part, :] * scale
        up_v[part, :] = (cot * active[part, :]).astype(BF)
        gate_v[part, :] = (cot * gate_factor[part, :]).astype(BF)
        return carry

    def make_grads():
        lax.fori_loop(0, SLOTS // 32, grads, 0)
        outs[0].start()
        outs[1].start()

    def product(i, carry):
        block = dot(moe_t[pl.ds(pl.multiple_of(i * 512, 512), 512), :], logit[...], 1, 1)
        prod[i] = block
        prod_b[i] = block.astype(BF)
        return carry

    def give_pair(k, carry):
        send(prod_b.at[2 * k + 1 - core], rp.at[k], rp_s, rp_r, sibling)
        return carry

    def router_terms():
        drain(back_recv.at[pl.ds(0, SLOTS - 16)], b_r)
        spread = (back_recv[...] * chooser).T
        high = spread.astype(BF)
        rest = spread - high.astype(F32)
        middle = rest.astype(BF)
        low = (rest - middle.astype(F32)).astype(BF)
        by_expert = dot(high, placer[...]) + dot(middle, placer[...]) + dot(low, placer[...])
        for k in range(TOPK):
            picked = jnp.where(ids[k : k + 1, :] == expert_row, by_expert, 0.0)
            route_v[k : k + 1, :] = jnp.sum(picked, 0, keepdims=True)
        outs[2].start()
        mine = weight_by_expert[...]
        mixed = jnp.sum(mine * by_expert, 0, keepdims=True)
        logit[...] = (mine * (by_expert - mixed)).astype(BF)
        lax.fori_loop(0, 8, product, 0)
        lax.fori_loop(0, 4, give_pair, 0)

    def pair_router(k, carry):
        both = prod[2 * k + core] + rp[k].astype(F32)
        rq_send[pl.ds(2 * k, 2)] = both.astype(BF).reshape(2, HALF, 128)
        return carry

    def give_plane(k, carry):
        target = plane(k)
        send(rq_send.at[:, pl.ds(m16(target), 16)], rq.at[yx], rq_s, rq_r, (d, zlo * 16 + target))
        return carry

    def router_pair():
        drain(rp, rp_r)
        lax.fori_loop(0, 4, pair_router, 0)
        rq[yx] = rq_send[:, pl.ds(m16(yx), 16), :]
        lax.fori_loop(1, 16, give_plane, 0)

    def add_plane(k, total):
        return total + rq[k].astype(F32)

    def give_column(k, carry):
        other, target = column(k)
        send(rz_send.at[other], rz.at[z], rz_s, rz_r, target)
        return carry

    def router_plane():
        drain(rq.at[pl.ds(0, 15)], rq_r)
        rz_send[...] = lax.fori_loop(1, 16, add_plane, rq[0].astype(F32)).astype(BF)
        rz[z] = rz_send[z]
        lax.fori_loop(1, 8, give_column, 0)

    def router_end():
        drain(rz.at[pl.ds(0, 7)], rz_r)
        total = rz[0].astype(F32)
        for k in range(1, 8):
            total = total + rz[k].astype(F32)
        router_v[...] = 0.015625 * total
        outs[3].start()

    pack(0, 0)
    pack(0, 1)
    make_gates()
    turn_moe()
    pack_partner(0)
    pack(0, 2)
    weigh_hidden()
    pack_partner(1)
    pack(0, 3)
    pack_partner(2)
    pack(0, 4)
    make_term(0)
    pack_partner(3)
    pack(0, 5)
    pair_sum(0)
    pack_partner(4)
    pack(0, 6)
    make_term(1)
    make_hidden(1)
    pack_partner(5)
    pack(0, 7)
    pair_sum(1)
    pack_partner(6)
    make_term(2)
    pack_partner(7)
    pair_sum(2)
    ring_step(0, 0)
    make_term(3)
    ring_step(1, 0)
    make_hidden(3)
    ring_step(2, 0)
    pair_sum(3)
    ring_step(0, 1)
    make_term(4)
    ring_step(1, 1)
    pair_sum(4)
    ring_step(2, 1)
    ring_step(3, 0)
    make_term(5)
    make_hidden(5)
    ring_end(0)
    pair_sum(5)
    ring_end(1)
    make_term(6)
    ring_step(4, 0)
    ring_end(2)
    make_term(7)
    pair_sum(6)
    make_hidden(7)
    ring_step(3, 1)
    give_dots()
    ring_step(5, 0)
    pair_sum(7)
    make_grads()
    ring_step(4, 1)
    ring_step(6, 0)
    ring_end(3)
    router_terms()
    ring_step(5, 1)
    ring_step(7, 0)
    router_pair()
    ring_end(4)
    ring_step(6, 1)
    ring_end(5)
    ring_step(7, 1)
    router_plane()
    ring_end(6)
    ring_end(7)
    router_end()
    drain(placer_p, z_s)
    drain(tok_p, z_s)
    drain(w_recv.at[pl.ds(0, SLOTS - 16)], w_s)
    drain(recv.at[pl.ds(0, SLOTS - 32)], a_s)
    drain(pair, p_s)
    drain(ring, g_s)
    drain(back_recv.at[pl.ds(0, SLOTS - 16)], b_s)
    drain(rp, rp_s)
    drain(rq.at[pl.ds(0, 15)], rq_s)
    drain(rz.at[pl.ds(0, 7)], rz_s)
    for copy in outs + down_outs:
        copy.wait()


def per_device(out_cot, route_ids, route_weight, saved_gate, saved_up, down_weight, moe_input):
    anywhere = pl.BlockSpec(memory_space=pl.ANY)
    dma = pltpu.SemaphoreType.DMA
    scratch = [
        ((TOK, D), BF),
        ((TOPK, TOK), jnp.int32),
        ((TOPK, TOK), F32),
        ((SLOTS, FFE), BF),
        ((SLOTS, FFE), BF),
        ((FFE, D), BF),
        ((TOK, D), BF),
        ((D, TOK), BF),
        ((SLOTS, TOK), BF),
        ((HALF, TOK), BF),
        ((TOK, D), BF),
        ((EXPERTS, TOK), F32),
        ((SLOTS, 128), BF),
        ((SLOTS, 128), BF),
        ((SLOTS, D), BF),
        ((SLOTS, D), BF),
        ((SLOTS, FFE), BF),
        ((SLOTS, FFE), F32),
        ((SLOTS, FFE), F32),
        ((FFE, SLOTS), BF),
        ((SLOTS, FFE), F32),
        ((4, 2, OWN, D), BF),
        ((4, OWN, D), BF),
        ((4, OWN, D), BF),
        ((3, OWN, D), BF),
        ((SLOTS, 128), F32),
        ((SLOTS, 128), F32),
        ((8, 512, 128), F32),
        ((8, 512, 128), BF),
        ((4, 512, 128), BF),
        ((8, HALF, 128), BF),
        ((16, 8, 16, 128), BF),
        ((8, 16, 128), BF),
        ((8, 16, 128), BF),
        ((SLOTS, FFE), BF),
        ((SLOTS, FFE), BF),
        ((OWN, D), F32),
        ((TOPK, TOK), F32),
        ((16, EXPERTS), F32),
    ]
    sems = [
        dma((7,)), dma(()), dma((NC + 1,)), dma(()), dma(()), dma(()), dma((NC, 2)),
        dma(()), dma((NC,)), dma(()), dma((NC, 3, 2)), dma(()), dma(()),
        dma(()), dma(()), dma(()), dma(()), dma(()), dma(()), dma((4 + NC,)),
        pltpu.VMEM((EXPERTS, TOK), BF),
    ]
    outs = pl.pallas_call(
        body,
        out_shape=(
            jax.ShapeDtypeStruct((SLOTS, FFE), BF),
            jax.ShapeDtypeStruct((SLOTS, FFE), BF),
            jax.ShapeDtypeStruct((OWN, D), F32),
            jax.ShapeDtypeStruct((TOPK, TOK), F32),
            jax.ShapeDtypeStruct((16, EXPERTS), F32),
        ),
        in_specs=[anywhere] * 7,
        out_specs=(anywhere,) * 5,
        scratch_shapes=[pltpu.VMEM(shape, kind) for shape, kind in scratch] + sems,
        compiler_params=pltpu.CompilerParams(
            collective_id=0, has_side_effects=True, vmem_limit_bytes=58 * 2**20
        ),
    )(
        out_cot, route_ids.T, route_weight.T, saved_gate[0, 0], saved_up[0, 0],
        down_weight[0], moe_input,
    )
    gate_grad, up_grad, down_grad, route_grad, router_grad = hand_over(outs)
    return gate_grad[None, None], up_grad[None, None], down_grad[None], route_grad.T, router_grad


def hand_over_body(*refs):
    sources, targets, held, load_sem, store_sem = refs[:5], refs[5:10], refs[10:15], refs[15], refs[16]
    loads, stores = [], []
    for source, target, here in zip(sources, targets, held):
        pieces = 4 if source.shape[0] >= 64 else 1
        rows = source.shape[0] // pieces
        for i in range(pieces):
            part, n = pl.ds(i * rows, rows), len(loads)
            loads.append(pltpu.make_async_copy(source.at[part], here.at[part], load_sem.at[n]))
            stores.append(pltpu.make_async_copy(here.at[part], target.at[part], store_sem.at[n]))
    for load in loads:
        load.start()
    for load, store in zip(loads, stores):
        load.wait()
        store.start()
    for store in stores:
        store.wait()


def hand_over(arrays):
    anywhere = pl.BlockSpec(memory_space=pl.ANY)
    return pl.pallas_call(
        hand_over_body,
        out_shape=[jax.ShapeDtypeStruct(a.shape, a.dtype) for a in arrays],
        in_specs=[anywhere] * 5,
        out_specs=[anywhere] * 5,
        scratch_shapes=[pltpu.VMEM(a.shape, a.dtype) for a in arrays]
        + [pltpu.SemaphoreType.DMA((14,))] * 2,
        compiler_params=pltpu.CompilerParams(vmem_limit_bytes=58 * 2**20),
    )(*arrays)


def solution(mesh):
    placed = (
        P(("dp", "expert"), None),
        P(("dp", "expert"), None),
        P(("dp", "expert"), None),
        P("dp", "expert", None, None),
        P("dp", "expert", None, None),
        P("expert", None, None),
        P(("dp", "expert"), None),
    )
    return jax.shard_map(
        per_device,
        mesh=mesh,
        in_specs=placed,
        out_specs=(
            P("dp", "expert", None, None),
            P("dp", "expert", None, None),
            P("expert", "dp", None),
            P(("dp", "expert"), None),
            P(("dp", "expert"), None),
        ),
        check_vma=False,
    )
```

```python
import functools

import jax
import jax.numpy as jnp
from jax import lax
from jax.experimental import pallas as pl
from jax.experimental.pallas import tpu as pltpu
from jax.sharding import PartitionSpec as P

EXP_DEV = 4
TOK = 128
TOPK = 8
D = 4096
FFE = 768
SLOTS = 512
HALF = SLOTS // 2
EXPERTS = 128
MOST = 16
NC = 8
DC = D // NC
DH = DC // 2
OWN = FFE // 8
MESH = pl.DeviceIdType.MESH
F32 = jnp.float32
BF = jnp.bfloat16


def dot(a, b, ca=1, cb=0):
    return lax.dot_general(a, b, (((ca,), (cb,)), ((), ())), preferred_element_type=F32)


def m16(index):
    return pl.multiple_of(index * 16, 16)


def body(
    tok_hbm, ids_hbm, rw_hbm, gate_hbm, up_hbm, w_hbm, moe_hbm,
    gate_out, up_out, down_out, route_out, router_out,
    tok, ids, rw, gate, up, w, moe, moe_t, placer, meta, meta_p, flying_code, tok_p, weight_by_expert,
    w_send, w_recv, snd, recv, hidden, active, gate_factor, hw_t, hc,
    term, pair, psum, ring, back_send, back_recv,
    prod, prod_b, rp, rq_send, rq, rz_send, rz, gate_v, up_v, down_v, route_v, router_v,
    in_sem, z_s, z_r, w_s, w_r, a_s, a_r, p_s, p_r, g_s, g_r, b_s, b_r,
    rp_s, rp_r, rq_s, rq_r, rz_s, rz_r, out_sem, logit,
):
    d = lax.axis_index("dp")
    e = lax.axis_index("expert")
    zhi, core = d // 2, d % 2
    zlo, yx = e // 16, e % 16
    y, x = yx // 4, yx % 4
    sibling = (zhi * 2 + 1 - core, e)
    partner = (d, (1 - zlo) * 16 + yx)
    up_ring = (((zhi + 1) % 4) * 2 + core, e)
    down_ring = (((zhi + 3) % 4) * 2 + core, e)
    z = zhi * 2 + zlo

    def column(k):
        other = (z + k) % 8
        return other, ((other // 2) * 2 + core, (other % 2) * 16 + yx)

    def plane(k):
        step = (k * 5) % 16
        return ((y + step // 4) % 4) * 4 + (x + step % 4) % 4

    def send(src, dst, s, r, target):
        pltpu.make_async_remote_copy(src, dst, s, r, target, MESH).start()

    def drain(ref, sem):
        pltpu.make_async_copy(ref, ref, sem).wait()

    bar = pltpu.get_barrier_semaphore()

    def greet(k, carry):
        pl.semaphore_signal(bar, inc=1, device_id=(d, (e + k) % 32), device_id_type=MESH)
        return carry

    lax.fori_loop(1, 32, greet, 0)
    pl.semaphore_signal(bar, inc=1, device_id=sibling, device_id_type=MESH)

    def greet_column(k, carry):
        pl.semaphore_signal(
            bar, inc=1, device_id=(((zhi + k) % 4) * 2 + core, e), device_id_type=MESH
        )
        pl.semaphore_signal(
            bar, inc=1, device_id=(((zhi + k) % 4) * 2 + core, (1 - zlo) * 16 + yx), device_id_type=MESH
        )
        return carry

    lax.fori_loop(1, 4, greet_column, 0)

    loads = [
        pltpu.make_async_copy(source, here, in_sem.at[i])
        for i, (source, here) in enumerate(
            (
                (ids_hbm, ids), (rw_hbm, rw), (tok_hbm, tok), (gate_hbm, gate),
                (up_hbm, up), (moe_hbm, moe), (w_hbm, w),
            )
        )
    ]
    for load in loads:
        load.start()
    load_ids, load_rw, load_tok, load_gate, load_up, load_moe, load_w = loads
    load_ids.wait()
    load_rw.wait()

    expert_row = lax.broadcasted_iota(jnp.int32, (EXPERTS, TOK), 0)
    token_lane = lax.broadcasted_iota(jnp.int32, (EXPERTS, TOK), 1)
    named = jnp.zeros((EXPERTS, TOK), F32)
    weights = jnp.zeros((EXPERTS, TOK), F32)
    for k in range(TOPK):
        match = ids[k : k + 1, :] == expert_row
        named = named + jnp.where(match, 1.0, 0.0)
        weights = weights + jnp.where(match, rw[k : k + 1, :], 0.0)
    weight_by_expert[...] = weights
    before = jnp.where(expert_row < token_lane, 1.0, 0.0).astype(BF)
    rank = dot(named.astype(BF), before)
    code = (named * (rank + 1.0)).astype(BF)
    flying_row = lax.broadcasted_iota(jnp.int32, (32, EXPERTS), 0)
    flying_lane = lax.broadcasted_iota(jnp.int32, (32, EXPERTS), 1)
    flying = jnp.where(flying_lane == EXP_DEV * flying_row, 1.0, 0.0).astype(BF)
    codes = dot(flying, code)
    flying_code[...] = codes
    flying_weight = dot(flying, weights.astype(BF)).astype(BF)
    meta[0, :16] = codes[:16].astype(BF)
    meta[0, 16:] = flying_weight[:16]
    meta[1, :16] = codes[16:].astype(BF)
    meta[1, 16:] = flying_weight[16:]

    half_row = lax.broadcasted_iota(jnp.int32, (HALF, 32), 0)
    half_lane = lax.broadcasted_iota(jnp.int32, (HALF, 32), 1)
    to_code = jnp.where(half_lane == half_row // MOST, 1.0, 0.0).astype(BF)
    to_weight = jnp.where(half_lane == 16 + half_row // MOST, 1.0, 0.0).astype(BF)
    place = (lax.broadcasted_iota(jnp.int32, (HALF, TOK), 0) % MOST + 1).astype(F32)

    def lay_out(half, about):
        placed = dot(to_code, about) == place
        placer[half] = jnp.where(placed, 1.0, 0.0).astype(BF)
        total = jnp.sum(jnp.where(placed, dot(to_weight, about), 0.0), 1, keepdims=True)
        w_send[half] = jnp.broadcast_to(total, (HALF, 128)).astype(BF)

    lay_out(0, meta[zlo])
    load_tok.wait()

    pl.semaphore_wait(bar, 38)

    send(meta.at[1 - zlo], meta_p, z_s, z_r.at[NC], partner)
    for c in range(NC):
        cols = pl.ds(c * DC, DC)
        send(tok.at[:, cols], tok_p.at[:, cols], z_s, z_r.at[c], partner)

    def pack(half, c):
        cols = pl.ds(c * DC, DC)
        chosen = placer[half]
        tokens = tok if half == 0 else tok_p
        for q in range(DC // 256):
            part = pl.ds(c * DC + q * 256, 256)
            snd[pl.ds(half * HALF, HALF), part] = dot(chosen, tokens[:, part]).astype(BF)
        source = zlo * 16 + yx if half == 0 else (1 - zlo) * 16 + yx
        recv[pl.ds(m16(source), 16), cols] = snd[pl.ds(m16(half * 16 + yx), 16), cols]

        def one(k, carry):
            target = plane(k)
            send(
                snd.at[pl.ds(m16(half * 16 + target), 16), cols],
                recv.at[pl.ds(m16(source), 16), cols],
                a_s, a_r.at[c, half], (d, zlo * 16 + target),
            )
            return carry

        lax.fori_loop(1, 16, one, 0)

    def give_weights(half):
        source = zlo * 16 + yx if half == 0 else (1 - zlo) * 16 + yx
        w_recv[pl.ds(m16(source), 16), :] = w_send[half, pl.ds(m16(yx), 16), :]

        def one(k, carry):
            target = plane(k)
            send(
                w_send.at[half, pl.ds(m16(target), 16)], w_recv.at[pl.ds(m16(source), 16)],
                w_s, w_r, (d, zlo * 16 + target),
            )
            return carry

        lax.fori_loop(1, 16, one, 0)

    def read_partner():
        drain(meta_p, z_r.at[NC])
        lay_out(1, meta_p[...])
        give_weights(1)

    def pack_partner(c):
        drain(tok_p.at[:, pl.ds(c * DC, DC)], z_r.at[c])
        pack(1, c)

    def gates(i, carry):
        part = pl.ds(pl.multiple_of(i * 32, 32), 32)
        g = gate[part, :].astype(F32)
        u = up[part, :].astype(F32)
        sigma = jax.nn.sigmoid(g)
        act = g * sigma
        active[part, :] = act
        gate_factor[part, :] = u * sigma * (1.0 + g * (1.0 - sigma))
        hidden[part, :] = (act * u).astype(BF)
        return carry

    def make_gates():
        load_gate.wait()
        load_up.wait()
        lax.fori_loop(0, SLOTS // 32, gates, 0)

    def turn(i, carry):
        part = pl.ds(pl.multiple_of(i * 512, 512), 512)
        moe_t[part, :] = moe[:, part].T
        return carry

    def turn_moe():
        load_moe.wait()
        lax.fori_loop(0, D // 512, turn, 0)

    def weigh(i, carry):
        part = pl.ds(pl.multiple_of(i * 128, 128), 128)
        scale = jnp.concatenate([w_recv[part, :].astype(F32)] * (FFE // 128), axis=1)
        hw_t[:, part] = (scale * hidden[part, :].astype(F32)).astype(BF).T
        return carry

    def weigh_hidden():
        drain(w_recv.at[pl.ds(0, SLOTS - 32)], w_r)
        lax.fori_loop(0, SLOTS // 128, weigh, 0)

    def arrive(c):
        for half in range(2):
            drain(recv.at[pl.ds(0, HALF - 16), pl.ds(c * DC, DC)], a_r.at[c, half])

    def make_term(c):
        arrive(c)
        for q in range(DC // 256):
            cols = pl.ds(c * DC + q * 256, 256)
            block = dot(hw_t[...], recv[:, cols]).astype(BF)
            term[:, :, :, cols] = block.reshape(4, 2, OWN, 256)
        cols = pl.ds(c * DC, DC)
        send(term.at[:, 1 - core, :, cols], pair.at[:, :, cols], p_s, p_r.at[c], sibling)

    def make_hidden(c):
        if c == 1:
            load_w.wait()
        cols = pl.ds((c - 1) * DC, 2 * DC)

        def one(q, carry):
            part = pl.ds(pl.multiple_of(q * 256, 256), 256)
            block = dot(recv[:, cols], w[part, cols], 1, 1)
            if c == 1:
                hc[:, part] = block
            else:
                hc[:, part] = hc[:, part] + block
            return carry

        lax.fori_loop(0, FFE // 256, one, 0)

    def ways(c):
        return (
            (0, pl.ds(c * DC, DH), up_ring, 1),
            (1, pl.ds(c * DC + DH, DH), down_ring, -1),
        )

    def pair_sum(c):
        cols = pl.ds(c * DC, DC)
        drain(pair.at[:, :, cols], p_r.at[c])

        def one(k, carry):
            both = term[k, core, :, cols].astype(F32) + pair[k, :, cols].astype(F32)
            psum[k, :, cols] = both.astype(BF)
            return carry

        lax.fori_loop(0, 4, one, 0)
        for way, part, target, sign in ways(c):
            block = (zhi + 4 - sign) % 4
            send(psum.at[block, :, part], ring.at[0, :, part], g_s, g_r.at[c, 0, way], target)

    def ring_step(c, step):
        for way, part, target, sign in ways(c):
            drain(ring.at[step, :, part], g_r.at[c, step, way])
            block = (zhi + 8 - sign * (step + 2)) % 4
            total = ring[step, :, part].astype(F32) + psum[block, :, part].astype(F32)
            ring[step, :, part] = total.astype(BF)
            send(ring.at[step, :, part], ring.at[step + 1, :, part], g_s, g_r.at[c, step + 1, way], target)

    outs = [
        pltpu.make_async_copy(gate_v, gate_out, out_sem.at[0]),
        pltpu.make_async_copy(up_v, up_out, out_sem.at[1]),
        pltpu.make_async_copy(route_v, route_out, out_sem.at[2]),
        pltpu.make_async_copy(router_v, router_out, out_sem.at[3]),
    ]
    down_outs = [
        pltpu.make_async_copy(
            down_v.at[:, pl.ds(c * DC, DC)], down_out.at[:, pl.ds(c * DC, DC)], out_sem.at[4 + c]
        )
        for c in range(NC)
    ]

    def ring_end(c):
        for way, part, target, sign in ways(c):
            drain(ring.at[2, :, part], g_r.at[c, 2, way])
            down_v[:, part] = ring[2, :, part].astype(F32) + psum[zhi, :, part].astype(F32)
        down_outs[c].start()

    def dots(i, carry):
        part = pl.ds(pl.multiple_of(i * 128, 128), 128)
        total = jnp.zeros((128, 128), F32)
        for q in range(FFE // 128):
            cols = pl.ds(q * 128, 128)
            total = total + hidden[part, cols].astype(F32) * hc[part, cols]
        back_send[i] = jnp.sum(total.T, 0, keepdims=True)
        return carry

    def give_back(k, carry):
        target = (e + k) % 32
        send(back_send.at[target // 8], back_recv.at[e], b_s, b_r, (d, target))
        return carry

    def give_dots():
        lax.fori_loop(0, SLOTS // 128, dots, 0)
        back_recv[e] = back_send[e // 8]
        lax.fori_loop(1, 32, give_back, 0)

    def grads(i, carry):
        part = pl.ds(pl.multiple_of(i * 32, 32), 32)
        scale = jnp.concatenate([w_recv[part, :].astype(F32)] * (FFE // 128), axis=1)
        cot = hc[part, :] * scale
        up_v[part, :] = (cot * active[part, :]).astype(BF)
        gate_v[part, :] = (cot * gate_factor[part, :]).astype(BF)
        return carry

    def make_grads():
        lax.fori_loop(0, SLOTS // 32, grads, 0)
        outs[0].start()
        outs[1].start()

    def product(i, carry):
        block = dot(moe_t[pl.ds(pl.multiple_of(i * 512, 512), 512), :], logit[...], 1, 1)
        prod[i] = block
        prod_b[i] = block.astype(BF)
        return carry

    def give_pair(k, carry):
        send(prod_b.at[2 * k + 1 - core], rp.at[k], rp_s, rp_r, sibling)
        return carry

    def router_terms():
        drain(back_recv.at[pl.ds(0, 31)], b_r)
        back = jnp.concatenate([back_recv[j] for j in range(32)], axis=0)
        back = pltpu.roll(back, (8 - e % 8) % 8 * 16, 1)
        flown = jnp.zeros((32, TOK), F32)
        for r in range(MOST):
            flown = flown + jnp.where(flying_code[...] == r + 1.0, back[:, r : r + 1], 0.0)
        stretch_row = lax.broadcasted_iota(jnp.int32, (EXPERTS, 32), 0)
        stretch_lane = lax.broadcasted_iota(jnp.int32, (EXPERTS, 32), 1)
        stretch = jnp.where(stretch_row == EXP_DEV * stretch_lane, 1.0, 0.0).astype(BF)
        high = flown.astype(BF)
        rest = flown - high.astype(F32)
        middle = rest.astype(BF)
        low = (rest - middle.astype(F32)).astype(BF)
        by_expert = dot(stretch, high) + dot(stretch, middle) + dot(stretch, low)
        for k in range(TOPK):
            picked = jnp.where(ids[k : k + 1, :] == expert_row, by_expert, 0.0)
            route_v[k : k + 1, :] = jnp.sum(picked, 0, keepdims=True)
        outs[2].start()
        mine = weight_by_expert[...]
        mixed = jnp.sum(mine * by_expert, 0, keepdims=True)
        logit[...] = (mine * (by_expert - mixed)).astype(BF)
        lax.fori_loop(0, 8, product, 0)
        lax.fori_loop(0, 4, give_pair, 0)

    def pair_router(k, carry):
        both = prod[2 * k + core] + rp[k].astype(F32)
        rq_send[pl.ds(2 * k, 2)] = both.astype(BF).reshape(2, HALF, 128)
        return carry

    def give_plane(k, carry):
        target = plane(k)
        send(rq_send.at[:, pl.ds(m16(target), 16)], rq.at[yx], rq_s, rq_r, (d, zlo * 16 + target))
        return carry

    def router_pair():
        drain(rp, rp_r)
        lax.fori_loop(0, 4, pair_router, 0)
        rq[yx] = rq_send[:, pl.ds(m16(yx), 16), :]
        lax.fori_loop(1, 16, give_plane, 0)

    def add_plane(k, total):
        return total + rq[k].astype(F32)

    def give_column(k, carry):
        other, target = column(k)
        send(rz_send.at[other], rz.at[z], rz_s, rz_r, target)
        return carry

    def router_plane():
        drain(rq.at[pl.ds(0, 15)], rq_r)
        rz_send[...] = lax.fori_loop(1, 16, add_plane, rq[0].astype(F32)).astype(BF)
        rz[z] = rz_send[z]
        lax.fori_loop(1, 8, give_column, 0)

    def router_end():
        drain(rz.at[pl.ds(0, 7)], rz_r)
        total = rz[0].astype(F32)
        for k in range(1, 8):
            total = total + rz[k].astype(F32)
        router_v[...] = 0.015625 * total
        outs[3].start()

    pack(0, 0)
    pack(0, 1)
    give_weights(0)
    make_gates()
    read_partner()
    turn_moe()
    pack_partner(0)
    pack(0, 2)
    weigh_hidden()
    pack_partner(1)
    pack(0, 3)
    pack_partner(2)
    pack(0, 4)
    make_term(0)
    pack_partner(3)
    pack(0, 5)
    pair_sum(0)
    pack_partner(4)
    pack(0, 6)
    make_term(1)
    make_hidden(1)
    pack_partner(5)
    pack(0, 7)
    pack_partner(6)
    pair_sum(1)
    make_term(2)
    pack_partner(7)
    ring_step(0, 0)
    pair_sum(2)
    ring_step(1, 0)
    make_term(3)
    make_hidden(3)
    ring_step(0, 1)
    ring_step(2, 0)
    pair_sum(3)
    ring_step(1, 1)
    make_term(4)
    ring_end(0)
    ring_step(2, 1)
    pair_sum(4)
    ring_step(3, 0)
    make_term(5)
    make_hidden(5)
    ring_end(1)
    ring_end(2)
    pair_sum(5)
    ring_step(4, 0)
    make_term(6)
    ring_step(3, 1)
    make_term(7)
    make_hidden(7)
    give_dots()
    pair_sum(6)
    ring_step(4, 1)
    pair_sum(7)
    ring_step(5, 0)
    ring_end(3)
    make_grads()
    router_terms()
    ring_step(6, 0)
    ring_end(4)
    ring_step(7, 0)
    router_pair()
    ring_step(5, 1)
    ring_step(6, 1)
    ring_step(7, 1)
    ring_end(5)
    router_plane()
    ring_end(6)
    ring_end(7)
    router_end()

    drain(meta_p, z_s)
    drain(tok_p, z_s)
    drain(w_recv.at[pl.ds(0, SLOTS - 32)], w_s)
    drain(recv.at[pl.ds(0, SLOTS - 32)], a_s)
    drain(pair, p_s)
    drain(ring, g_s)
    drain(back_recv.at[pl.ds(0, 31)], b_s)
    drain(rp, rp_s)
    drain(rq.at[pl.ds(0, 15)], rq_s)
    drain(rz.at[pl.ds(0, 7)], rz_s)
    for copy in outs + down_outs:
        copy.wait()


def per_device(out_cot, route_ids, route_weight, saved_gate, saved_up, down_weight, moe_input):
    anywhere = pl.BlockSpec(memory_space=pl.ANY)
    dma = pltpu.SemaphoreType.DMA
    scratch = [
        ((TOK, D), BF),
        ((TOPK, TOK), jnp.int32),
        ((TOPK, TOK), F32),
        ((SLOTS, FFE), BF),
        ((SLOTS, FFE), BF),
        ((FFE, D), BF),
        ((TOK, D), BF),
        ((D, TOK), BF),
        ((2, HALF, TOK), BF),
        ((2, 32, TOK), BF),
        ((32, TOK), BF),
        ((32, TOK), F32),
        ((TOK, D), BF),
        ((EXPERTS, TOK), F32),
        ((2, HALF, 128), BF),
        ((SLOTS, 128), BF),
        ((SLOTS, D), BF),
        ((SLOTS, D), BF),
        ((SLOTS, FFE), BF),
        ((SLOTS, FFE), F32),
        ((SLOTS, FFE), F32),
        ((FFE, SLOTS), BF),
        ((SLOTS, FFE), F32),
        ((4, 2, OWN, D), BF),
        ((4, OWN, D), BF),
        ((4, OWN, D), BF),
        ((3, OWN, D), BF),
        ((4, 1, 128), F32),
        ((32, 1, 128), F32),
        ((8, 512, 128), F32),
        ((8, 512, 128), BF),
        ((4, 512, 128), BF),
        ((8, HALF, 128), BF),
        ((16, 8, 16, 128), BF),
        ((8, 16, 128), BF),
        ((8, 16, 128), BF),
        ((SLOTS, FFE), BF),
        ((SLOTS, FFE), BF),
        ((OWN, D), F32),
        ((TOPK, TOK), F32),
        ((16, EXPERTS), F32),
    ]
    sems = [
        dma((7,)), dma(()), dma((NC + 1,)), dma(()), dma(()), dma(()), dma((NC, 2)),
        dma(()), dma((NC,)), dma(()), dma((NC, 3, 2)), dma(()), dma(()),
        dma(()), dma(()), dma(()), dma(()), dma(()), dma(()), dma((4 + NC,)),
        pltpu.VMEM((EXPERTS, TOK), BF),
    ]
    outs = pl.pallas_call(
        body,
        out_shape=(
            jax.ShapeDtypeStruct((SLOTS, FFE), BF),
            jax.ShapeDtypeStruct((SLOTS, FFE), BF),
            jax.ShapeDtypeStruct((OWN, D), F32),
            jax.ShapeDtypeStruct((TOPK, TOK), F32),
            jax.ShapeDtypeStruct((16, EXPERTS), F32),
        ),
        in_specs=[anywhere] * 7,
        out_specs=(anywhere,) * 5,
        scratch_shapes=[pltpu.VMEM(shape, kind) for shape, kind in scratch] + sems,
        compiler_params=pltpu.CompilerParams(
            collective_id=0, has_side_effects=True, vmem_limit_bytes=58 * 2**20
        ),
    )(
        out_cot, route_ids.T, route_weight.T, saved_gate[0, 0], saved_up[0, 0],
        down_weight[0], moe_input,
    )
    gate_grad, up_grad, down_grad, route_grad, router_grad = hand_over(outs)
    return gate_grad[None, None], up_grad[None, None], down_grad[None], route_grad.T, router_grad


def hand_over_body(*refs):
    sources, targets, held, load_sem, store_sem = refs[:5], refs[5:10], refs[10:15], refs[15], refs[16]
    loads, stores = [], []
    for source, target, here in zip(sources, targets, held):
        pieces = 4 if source.shape[0] >= 64 else 1
        rows = source.shape[0] // pieces
        for i in range(pieces):
            part, n = pl.ds(i * rows, rows), len(loads)
            loads.append(pltpu.make_async_copy(source.at[part], here.at[part], load_sem.at[n]))
            stores.append(pltpu.make_async_copy(here.at[part], target.at[part], store_sem.at[n]))
    for load in loads:
        load.start()
    for load, store in zip(loads, stores):
        load.wait()
        store.start()
    for store in stores:
        store.wait()


def hand_over(arrays):
    anywhere = pl.BlockSpec(memory_space=pl.ANY)
    return pl.pallas_call(
        hand_over_body,
        out_shape=[jax.ShapeDtypeStruct(a.shape, a.dtype) for a in arrays],
        in_specs=[anywhere] * 5,
        out_specs=[anywhere] * 5,
        scratch_shapes=[pltpu.VMEM(a.shape, a.dtype) for a in arrays]
        + [pltpu.SemaphoreType.DMA((14,))] * 2,
        compiler_params=pltpu.CompilerParams(vmem_limit_bytes=58 * 2**20),
    )(*arrays)


def solution(mesh):
    placed = (
        P(("dp", "expert"), None),
        P(("dp", "expert"), None),
        P(("dp", "expert"), None),
        P("dp", "expert", None, None),
        P("dp", "expert", None, None),
        P("expert", None, None),
        P(("dp", "expert"), None),
    )
    return jax.shard_map(
        per_device,
        mesh=mesh,
        in_specs=placed,
        out_specs=(
            P("dp", "expert", None, None),
            P("dp", "expert", None, None),
            P("expert", "dp", None),
            P(("dp", "expert"), None),
            P(("dp", "expert"), None),
        ),
        check_vma=False,
    )
```

```python
import functools

import jax
import jax.numpy as jnp
from jax import lax
from jax.experimental import pallas as pl
from jax.experimental.pallas import tpu as pltpu
from jax.sharding import PartitionSpec as P

EXP_DEV = 4
TOK = 128
TOPK = 8
D = 4096
FFE = 768
SLOTS = 512
HALF = SLOTS // 2
EXPERTS = 128
MOST = 16
NC = 8
DC = D // NC
DH = DC // 2
OWN = FFE // 8
MESH = pl.DeviceIdType.MESH
F32 = jnp.float32
BF = jnp.bfloat16


def dot(a, b, ca=1, cb=0):
    return lax.dot_general(a, b, (((ca,), (cb,)), ((), ())), preferred_element_type=F32)


def m16(index):
    return pl.multiple_of(index * 16, 16)


def body(
    tok_hbm, ids_hbm, rw_hbm, gate_hbm, up_hbm, w_hbm, moe_hbm,
    gate_out, up_out, down_out, route_out, router_out,
    tok, ids, rw, gate, up, w, moe, moe_t, placer, meta, meta_p, flying_code, tok_p, weight_by_expert,
    w_send, w_recv, snd, recv, hidden, active, gate_factor, hw_t, hc,
    term, pair, psum, ring, back_send, back_recv,
    prod, prod_b, rp, rq_send, rq, rz_send, rz, gate_v, up_v, down_v, route_v, router_v,
    in_sem, z_s, z_r, w_s, w_r, a_s, a_r, p_s, p_r, g_s, g_r, b_s, b_r,
    rp_s, rp_r, rq_s, rq_r, rz_s, rz_r, out_sem, logit,
):
    d = lax.axis_index("dp")
    e = lax.axis_index("expert")
    zhi, core = d // 2, d % 2
    zlo, yx = e // 16, e % 16
    y, x = yx // 4, yx % 4
    sibling = (zhi * 2 + 1 - core, e)
    partner = (d, (1 - zlo) * 16 + yx)
    up_ring = (((zhi + 1) % 4) * 2 + core, e)
    down_ring = (((zhi + 3) % 4) * 2 + core, e)
    z = zhi * 2 + zlo

    def column(k):
        other = (z + k) % 8
        return other, ((other // 2) * 2 + core, (other % 2) * 16 + yx)

    def plane(k):
        step = (k * 5) % 16
        return ((y + step // 4) % 4) * 4 + (x + step % 4) % 4

    def send(src, dst, s, r, target):
        pltpu.make_async_remote_copy(src, dst, s, r, target, MESH).start()

    def drain(ref, sem):
        pltpu.make_async_copy(ref, ref, sem).wait()

    bar = pltpu.get_barrier_semaphore()

    def greet(k, carry):
        pl.semaphore_signal(bar, inc=1, device_id=(d, (e + k) % 32), device_id_type=MESH)
        return carry

    lax.fori_loop(1, 32, greet, 0)
    pl.semaphore_signal(bar, inc=1, device_id=sibling, device_id_type=MESH)

    def greet_column(k, carry):
        pl.semaphore_signal(
            bar, inc=1, device_id=(((zhi + k) % 4) * 2 + core, e), device_id_type=MESH
        )
        pl.semaphore_signal(
            bar, inc=1, device_id=(((zhi + k) % 4) * 2 + core, (1 - zlo) * 16 + yx), device_id_type=MESH
        )
        return carry

    lax.fori_loop(1, 4, greet_column, 0)

    loads = [
        pltpu.make_async_copy(source, here, in_sem.at[i])
        for i, (source, here) in enumerate(
            (
                (ids_hbm, ids), (rw_hbm, rw), (tok_hbm, tok), (gate_hbm, gate),
                (up_hbm, up), (moe_hbm, moe), (w_hbm, w),
            )
        )
    ]
    for load in loads:
        load.start()
    load_ids, load_rw, load_tok, load_gate, load_up, load_moe, load_w = loads
    load_ids.wait()
    load_rw.wait()

    expert_row = lax.broadcasted_iota(jnp.int32, (EXPERTS, TOK), 0)
    token_lane = lax.broadcasted_iota(jnp.int32, (EXPERTS, TOK), 1)
    named = jnp.zeros((EXPERTS, TOK), F32)
    weights = jnp.zeros((EXPERTS, TOK), F32)
    for k in range(TOPK):
        match = ids[k : k + 1, :] == expert_row
        named = named + jnp.where(match, 1.0, 0.0)
        weights = weights + jnp.where(match, rw[k : k + 1, :], 0.0)
    weight_by_expert[...] = weights
    before = jnp.where(expert_row < token_lane, 1.0, 0.0).astype(BF)
    rank = dot(named.astype(BF), before)
    code = (named * (rank + 1.0)).astype(BF)
    flying_row = lax.broadcasted_iota(jnp.int32, (32, EXPERTS), 0)
    flying_lane = lax.broadcasted_iota(jnp.int32, (32, EXPERTS), 1)
    flying = jnp.where(flying_lane == EXP_DEV * flying_row, 1.0, 0.0).astype(BF)
    codes = dot(flying, code)
    flying_code[...] = codes
    flying_weight = dot(flying, weights.astype(BF)).astype(BF)
    meta[0, :16] = codes[:16].astype(BF)
    meta[0, 16:] = flying_weight[:16]
    meta[1, :16] = codes[16:].astype(BF)
    meta[1, 16:] = flying_weight[16:]

    half_row = lax.broadcasted_iota(jnp.int32, (HALF, 32), 0)
    half_lane = lax.broadcasted_iota(jnp.int32, (HALF, 32), 1)
    to_code = jnp.where(half_lane == half_row // MOST, 1.0, 0.0).astype(BF)
    to_weight = jnp.where(half_lane == 16 + half_row // MOST, 1.0, 0.0).astype(BF)
    place = (lax.broadcasted_iota(jnp.int32, (HALF, TOK), 0) % MOST + 1).astype(F32)

    def lay_out(half, about):
        placed = dot(to_code, about) == place
        placer[half] = jnp.where(placed, 1.0, 0.0).astype(BF)
        total = jnp.sum(jnp.where(placed, dot(to_weight, about), 0.0), 1, keepdims=True)
        w_send[half] = jnp.broadcast_to(total, (HALF, 128)).astype(BF)

    lay_out(0, meta[zlo])
    load_tok.wait()

    pl.semaphore_wait(bar, 38)

    send(meta.at[1 - zlo], meta_p, z_s, z_r.at[NC], partner)
    for c in range(NC):
        cols = pl.ds(c * DC, DC)
        send(tok.at[:, cols], tok_p.at[:, cols], z_s, z_r.at[c], partner)

    def pack(half, c):
        cols = pl.ds(c * DC, DC)
        chosen = placer[half]
        tokens = tok if half == 0 else tok_p
        for q in range(DC // 256):
            part = pl.ds(c * DC + q * 256, 256)
            snd[pl.ds(half * HALF, HALF), part] = dot(chosen, tokens[:, part]).astype(BF)
        source = zlo * 16 + yx if half == 0 else (1 - zlo) * 16 + yx
        recv[pl.ds(m16(source), 16), cols] = snd[pl.ds(m16(half * 16 + yx), 16), cols]

        def one(k, carry):
            target = plane(k)
            send(
                snd.at[pl.ds(m16(half * 16 + target), 16), cols],
                recv.at[pl.ds(m16(source), 16), cols],
                a_s, a_r.at[c, half], (d, zlo * 16 + target),
            )
            return carry

        lax.fori_loop(1, 16, one, 0)

    def give_weights(half):
        source = zlo * 16 + yx if half == 0 else (1 - zlo) * 16 + yx
        w_recv[pl.ds(m16(source), 16), :] = w_send[half, pl.ds(m16(yx), 16), :]

        def one(k, carry):
            target = plane(k)
            send(
                w_send.at[half, pl.ds(m16(target), 16)], w_recv.at[pl.ds(m16(source), 16)],
                w_s, w_r, (d, zlo * 16 + target),
            )
            return carry

        lax.fori_loop(1, 16, one, 0)

    def read_partner():
        drain(meta_p, z_r.at[NC])
        lay_out(1, meta_p[...])
        give_weights(1)

    def pack_partner(c):
        drain(tok_p.at[:, pl.ds(c * DC, DC)], z_r.at[c])
        pack(1, c)

    def gates(i, carry):
        part = pl.ds(pl.multiple_of(i * 32, 32), 32)
        g = gate[part, :].astype(F32)
        u = up[part, :].astype(F32)
        sigma = jax.nn.sigmoid(g)
        act = g * sigma
        active[part, :] = act
        gate_factor[part, :] = u * sigma * (1.0 + g * (1.0 - sigma))
        hidden[part, :] = (act * u).astype(BF)
        return carry

    def make_gates():
        load_gate.wait()
        load_up.wait()
        lax.fori_loop(0, SLOTS // 32, gates, 0)

    def turn(i, carry):
        part = pl.ds(pl.multiple_of(i * 512, 512), 512)
        moe_t[part, :] = moe[:, part].T
        return carry

    def turn_moe():
        load_moe.wait()
        lax.fori_loop(0, D // 512, turn, 0)

    def weigh(i, carry):
        part = pl.ds(pl.multiple_of(i * 128, 128), 128)
        scale = jnp.concatenate([w_recv[part, :].astype(F32)] * (FFE // 128), axis=1)
        hw_t[:, part] = (scale * hidden[part, :].astype(F32)).astype(BF).T
        return carry

    def weigh_hidden():
        drain(w_recv.at[pl.ds(0, SLOTS - 32)], w_r)
        lax.fori_loop(0, SLOTS // 128, weigh, 0)

    def arrive(c):
        for half in range(2):
            drain(recv.at[pl.ds(0, HALF - 16), pl.ds(c * DC, DC)], a_r.at[c, half])

    def make_term(c):
        arrive(c)
        for q in range(DC // 256):
            cols = pl.ds(c * DC + q * 256, 256)
            block = dot(hw_t[...], recv[:, cols]).astype(BF)
            term[:, :, :, cols] = block.reshape(4, 2, OWN, 256)
        cols = pl.ds(c * DC, DC)
        send(term.at[:, 1 - core, :, cols], pair.at[:, :, cols], p_s, p_r.at[c], sibling)

    def make_hidden(c):
        if c == 1:
            load_w.wait()
        first = c - 1 if c < NC - 2 else c
        cols = pl.ds(first * DC, (c + 1 - first) * DC)

        def one(q, carry):
            part = pl.ds(pl.multiple_of(q * 256, 256), 256)
            block = dot(recv[:, cols], w[part, cols], 1, 1)
            if c == 1:
                hc[:, part] = block
            else:
                hc[:, part] = hc[:, part] + block
            return carry

        lax.fori_loop(0, FFE // 256, one, 0)

    def ways(c):
        return (
            (0, pl.ds(c * DC, DH), up_ring, 1),
            (1, pl.ds(c * DC + DH, DH), down_ring, -1),
        )

    def pair_sum(c):
        cols = pl.ds(c * DC, DC)
        drain(pair.at[:, :, cols], p_r.at[c])

        def one(k, carry):
            both = term[k, core, :, cols].astype(F32) + pair[k, :, cols].astype(F32)
            psum[k, :, cols] = both.astype(BF)
            return carry

        lax.fori_loop(0, 4, one, 0)
        for way, part, target, sign in ways(c):
            block = (zhi + 4 - sign) % 4
            send(psum.at[block, :, part], ring.at[0, :, part], g_s, g_r.at[c, 0, way], target)

    def ring_step(c, step):
        for way, part, target, sign in ways(c):
            drain(ring.at[step, :, part], g_r.at[c, step, way])
            block = (zhi + 8 - sign * (step + 2)) % 4
            total = ring[step, :, part].astype(F32) + psum[block, :, part].astype(F32)
            ring[step, :, part] = total.astype(BF)
            send(ring.at[step, :, part], ring.at[step + 1, :, part], g_s, g_r.at[c, step + 1, way], target)

    outs = [
        pltpu.make_async_copy(gate_v, gate_out, out_sem.at[0]),
        pltpu.make_async_copy(up_v, up_out, out_sem.at[1]),
        pltpu.make_async_copy(route_v, route_out, out_sem.at[2]),
        pltpu.make_async_copy(router_v, router_out, out_sem.at[3]),
    ]
    down_outs = [
        pltpu.make_async_copy(
            down_v.at[:, pl.ds(c * DC, DC)], down_out.at[:, pl.ds(c * DC, DC)], out_sem.at[4 + c]
        )
        for c in range(NC)
    ]

    def ring_end(c):
        for way, part, target, sign in ways(c):
            drain(ring.at[2, :, part], g_r.at[c, 2, way])
            down_v[:, part] = ring[2, :, part].astype(F32) + psum[zhi, :, part].astype(F32)
        down_outs[c].start()

    def dots(i, carry):
        part = pl.ds(pl.multiple_of(i * 128, 128), 128)
        total = jnp.zeros((128, 128), F32)
        for q in range(FFE // 128):
            cols = pl.ds(q * 128, 128)
            total = total + hidden[part, cols].astype(F32) * hc[part, cols]
        back_send[i] = jnp.sum(total.T, 0, keepdims=True)
        return carry

    def give_back(k, carry):
        target = (e + k) % 32
        send(back_send.at[target // 8], back_recv.at[e], b_s, b_r, (d, target))
        return carry

    def give_dots():
        lax.fori_loop(0, SLOTS // 128, dots, 0)
        back_recv[e] = back_send[e // 8]
        lax.fori_loop(1, 32, give_back, 0)

    def grads(i, carry):
        part = pl.ds(pl.multiple_of(i * 32, 32), 32)
        scale = jnp.concatenate([w_recv[part, :].astype(F32)] * (FFE // 128), axis=1)
        cot = hc[part, :] * scale
        up_v[part, :] = (cot * active[part, :]).astype(BF)
        gate_v[part, :] = (cot * gate_factor[part, :]).astype(BF)
        return carry

    def make_grads():
        lax.fori_loop(0, SLOTS // 32, grads, 0)
        outs[0].start()
        outs[1].start()

    def product(i):
        return dot(moe_t[pl.ds(pl.multiple_of(i * 512, 512), 512), :], logit[...], 1, 1)

    def product_sibling(k, carry):
        prod_b[k] = product(2 * k + 1 - core).astype(BF)
        send(prod_b.at[k], rp.at[k], rp_s, rp_r, sibling)
        return carry

    def product_own(k, carry):
        prod[k] = product(2 * k + core)
        return carry

    def router_terms():
        drain(back_recv.at[pl.ds(0, 31)], b_r)
        back = jnp.concatenate([back_recv[j] for j in range(32)], axis=0)
        back = pltpu.roll(back, (8 - e % 8) % 8 * 16, 1)
        flown = jnp.zeros((32, TOK), F32)
        for r in range(MOST):
            flown = flown + jnp.where(flying_code[...] == r + 1.0, back[:, r : r + 1], 0.0)
        stretch_row = lax.broadcasted_iota(jnp.int32, (EXPERTS, 32), 0)
        stretch_lane = lax.broadcasted_iota(jnp.int32, (EXPERTS, 32), 1)
        stretch = jnp.where(stretch_row == EXP_DEV * stretch_lane, 1.0, 0.0).astype(BF)
        high = flown.astype(BF)
        rest = flown - high.astype(F32)
        middle = rest.astype(BF)
        low = (rest - middle.astype(F32)).astype(BF)
        by_expert = dot(stretch, high) + dot(stretch, middle) + dot(stretch, low)
        for k in range(TOPK):
            picked = jnp.where(ids[k : k + 1, :] == expert_row, by_expert, 0.0)
            route_v[k : k + 1, :] = jnp.sum(picked, 0, keepdims=True)
        outs[2].start()
        mine = weight_by_expert[...]
        mixed = jnp.sum(mine * by_expert, 0, keepdims=True)
        logit[...] = (mine * (by_expert - mixed)).astype(BF)
        lax.fori_loop(0, 4, product_sibling, 0)
        lax.fori_loop(0, 4, product_own, 0)

    def pair_router(k, carry):
        both = prod[k] + rp[k].astype(F32)
        rq_send[pl.ds(2 * k, 2)] = both.astype(BF).reshape(2, HALF, 128)
        return carry

    def give_plane(k, carry):
        target = plane(k)
        send(rq_send.at[:, pl.ds(m16(target), 16)], rq.at[yx], rq_s, rq_r, (d, zlo * 16 + target))
        return carry

    def router_pair():
        drain(rp, rp_r)
        lax.fori_loop(0, 4, pair_router, 0)
        rq[yx] = rq_send[:, pl.ds(m16(yx), 16), :]
        lax.fori_loop(1, 16, give_plane, 0)

    def add_plane(k, total):
        return total + rq[k].astype(F32)

    def give_column(k, carry):
        other, target = column(k)
        send(rz_send.at[other], rz.at[z], rz_s, rz_r, target)
        return carry

    def router_plane():
        drain(rq.at[pl.ds(0, 15)], rq_r)
        rz_send[...] = lax.fori_loop(1, 16, add_plane, rq[0].astype(F32)).astype(BF)
        rz[z] = rz_send[z]
        lax.fori_loop(1, 8, give_column, 0)

    def router_end():
        drain(rz.at[pl.ds(0, 7)], rz_r)
        total = rz[0].astype(F32)
        for k in range(1, 8):
            total = total + rz[k].astype(F32)
        router_v[...] = 0.015625 * total
        outs[3].start()

    pack(0, 0)
    pack(0, 1)
    give_weights(0)
    make_gates()
    read_partner()
    turn_moe()
    pack_partner(0)
    pack(0, 2)
    weigh_hidden()
    pack_partner(1)
    pack(0, 3)
    pack_partner(2)
    pack(0, 4)
    make_term(0)
    pack_partner(3)
    pack(0, 5)
    pair_sum(0)
    pack_partner(4)
    pack(0, 6)
    make_term(1)
    make_hidden(1)
    pack_partner(5)
    pack(0, 7)
    pack_partner(6)
    make_term(2)
    pair_sum(1)
    pack_partner(7)
    pair_sum(2)
    ring_step(0, 0)
    make_term(3)
    make_hidden(3)
    ring_step(1, 0)
    ring_step(2, 0)
    pair_sum(3)
    ring_step(0, 1)
    make_term(4)
    ring_step(1, 1)
    ring_step(2, 1)
    pair_sum(4)
    make_term(5)
    make_hidden(5)
    ring_step(3, 0)
    pair_sum(5)
    ring_end(0)
    make_term(6)
    make_hidden(6)
    ring_end(1)
    make_term(7)
    make_hidden(7)
    give_dots()
    pair_sum(6)
    ring_step(3, 1)
    ring_step(4, 0)
    pair_sum(7)
    ring_step(5, 0)
    ring_end(2)
    make_grads()
    router_terms()
    ring_step(6, 0)
    ring_step(4, 1)
    router_pair()
    ring_end(3)
    ring_step(7, 0)
    ring_step(5, 1)
    ring_step(6, 1)
    router_plane()
    ring_step(7, 1)
    ring_end(4)
    router_end()
    ring_end(5)
    ring_end(6)
    ring_end(7)

    drain(meta_p, z_s)
    drain(tok_p, z_s)
    drain(w_recv.at[pl.ds(0, SLOTS - 32)], w_s)
    drain(recv.at[pl.ds(0, SLOTS - 32)], a_s)
    drain(pair, p_s)
    drain(ring, g_s)
    drain(back_recv.at[pl.ds(0, 31)], b_s)
    drain(rp, rp_s)
    drain(rq.at[pl.ds(0, 15)], rq_s)
    drain(rz.at[pl.ds(0, 7)], rz_s)
    for copy in outs + down_outs:
        copy.wait()


def per_device(out_cot, route_ids, route_weight, saved_gate, saved_up, down_weight, moe_input):
    anywhere = pl.BlockSpec(memory_space=pl.ANY)
    dma = pltpu.SemaphoreType.DMA
    scratch = [
        ((TOK, D), BF),
        ((TOPK, TOK), jnp.int32),
        ((TOPK, TOK), F32),
        ((SLOTS, FFE), BF),
        ((SLOTS, FFE), BF),
        ((FFE, D), BF),
        ((TOK, D), BF),
        ((D, TOK), BF),
        ((2, HALF, TOK), BF),
        ((2, 32, TOK), BF),
        ((32, TOK), BF),
        ((32, TOK), F32),
        ((TOK, D), BF),
        ((EXPERTS, TOK), F32),
        ((2, HALF, 128), BF),
        ((SLOTS, 128), BF),
        ((SLOTS, D), BF),
        ((SLOTS, D), BF),
        ((SLOTS, FFE), BF),
        ((SLOTS, FFE), F32),
        ((SLOTS, FFE), F32),
        ((FFE, SLOTS), BF),
        ((SLOTS, FFE), F32),
        ((4, 2, OWN, D), BF),
        ((4, OWN, D), BF),
        ((4, OWN, D), BF),
        ((3, OWN, D), BF),
        ((4, 1, 128), F32),
        ((32, 1, 128), F32),
        ((4, 512, 128), F32),
        ((4, 512, 128), BF),
        ((4, 512, 128), BF),
        ((8, HALF, 128), BF),
        ((16, 8, 16, 128), BF),
        ((8, 16, 128), BF),
        ((8, 16, 128), BF),
        ((SLOTS, FFE), BF),
        ((SLOTS, FFE), BF),
        ((OWN, D), F32),
        ((TOPK, TOK), F32),
        ((16, EXPERTS), F32),
    ]
    sems = [
        dma((7,)), dma(()), dma((NC + 1,)), dma(()), dma(()), dma(()), dma((NC, 2)),
        dma(()), dma((NC,)), dma(()), dma((NC, 3, 2)), dma(()), dma(()),
        dma(()), dma(()), dma(()), dma(()), dma(()), dma(()), dma((4 + NC,)),
        pltpu.VMEM((EXPERTS, TOK), BF),
    ]
    outs = pl.pallas_call(
        body,
        out_shape=(
            jax.ShapeDtypeStruct((SLOTS, FFE), BF),
            jax.ShapeDtypeStruct((SLOTS, FFE), BF),
            jax.ShapeDtypeStruct((OWN, D), F32),
            jax.ShapeDtypeStruct((TOPK, TOK), F32),
            jax.ShapeDtypeStruct((16, EXPERTS), F32),
        ),
        in_specs=[anywhere] * 7,
        out_specs=(anywhere,) * 5,
        scratch_shapes=[pltpu.VMEM(shape, kind) for shape, kind in scratch] + sems,
        compiler_params=pltpu.CompilerParams(
            collective_id=0, has_side_effects=True, vmem_limit_bytes=58 * 2**20
        ),
    )(
        out_cot, route_ids.T, route_weight.T, saved_gate[0, 0], saved_up[0, 0],
        down_weight[0], moe_input,
    )
    gate_grad, up_grad, down_grad, route_grad, router_grad = hand_over(outs)
    return gate_grad[None, None], up_grad[None, None], down_grad[None], route_grad.T, router_grad


def hand_over_body(*refs):
    sources, targets, held, load_sem, store_sem = refs[:5], refs[5:10], refs[10:15], refs[15], refs[16]
    loads, stores = [], []
    for source, target, here in zip(sources, targets, held):
        pieces = 4 if source.shape[0] >= 64 else 1
        rows = source.shape[0] // pieces
        for i in range(pieces):
            part, n = pl.ds(i * rows, rows), len(loads)
            loads.append(pltpu.make_async_copy(source.at[part], here.at[part], load_sem.at[n]))
            stores.append(pltpu.make_async_copy(here.at[part], target.at[part], store_sem.at[n]))
    for load in loads:
        load.start()
    for load, store in zip(loads, stores):
        load.wait()
        store.start()
    for store in stores:
        store.wait()


def hand_over(arrays):
    anywhere = pl.BlockSpec(memory_space=pl.ANY)
    return pl.pallas_call(
        hand_over_body,
        out_shape=[jax.ShapeDtypeStruct(a.shape, a.dtype) for a in arrays],
        in_specs=[anywhere] * 5,
        out_specs=[anywhere] * 5,
        scratch_shapes=[pltpu.VMEM(a.shape, a.dtype) for a in arrays]
        + [pltpu.SemaphoreType.DMA((14,))] * 2,
        compiler_params=pltpu.CompilerParams(vmem_limit_bytes=58 * 2**20),
    )(*arrays)


def solution(mesh):
    placed = (
        P(("dp", "expert"), None),
        P(("dp", "expert"), None),
        P(("dp", "expert"), None),
        P("dp", "expert", None, None),
        P("dp", "expert", None, None),
        P("expert", None, None),
        P(("dp", "expert"), None),
    )
    return jax.shard_map(
        per_device,
        mesh=mesh,
        in_specs=placed,
        out_specs=(
            P("dp", "expert", None, None),
            P("dp", "expert", None, None),
            P("expert", "dp", None),
            P(("dp", "expert"), None),
            P(("dp", "expert"), None),
        ),
        check_vma=False,
    )
```

```python
import functools

import jax
import jax.numpy as jnp
from jax import lax
from jax.experimental import pallas as pl
from jax.experimental.pallas import tpu as pltpu
from jax.sharding import PartitionSpec as P

EXP_DEV = 4
TOK = 128
TOPK = 8
D = 4096
FFE = 768
SLOTS = 512
HALF = SLOTS // 2
EXPERTS = 128
MOST = 16
NC = 8
DC = D // NC
DH = DC // 2
OWN = FFE // 8
MESH = pl.DeviceIdType.MESH
F32 = jnp.float32
BF = jnp.bfloat16


def dot(a, b, ca=1, cb=0):
    return lax.dot_general(a, b, (((ca,), (cb,)), ((), ())), preferred_element_type=F32)


def m16(index):
    return pl.multiple_of(index * 16, 16)


def body(
    tok_hbm, ids_hbm, rw_hbm, gate_hbm, up_hbm, w_hbm, moe_hbm,
    gate_out, up_out, down_out, route_out, router_out,
    tok, ids, rw, gate, up, w, moe, moe_t, placer, meta, meta_p, flying_code, tok_p, weight_by_expert,
    w_send, w_recv, snd, recv, hidden, active, gate_factor, hw_t, hc,
    term, pair, psum, ring, back_send, back_recv,
    prod, prod_b, rp, rq_send, rq, rz_send, rz, gate_v, up_v, down_v, route_v, router_v,
    in_sem, z_s, z_r, w_s, w_r, a_s, a_r, p_s, p_r, g_s, g_r, b_s, b_r,
    rp_s, rp_r, rq_s, rq_r, rz_s, rz_r, out_sem, logit,
):
    d = lax.axis_index("dp")
    e = lax.axis_index("expert")
    zhi, core = d // 2, d % 2
    zlo, yx = e // 16, e % 16
    y, x = yx // 4, yx % 4
    sibling = (zhi * 2 + 1 - core, e)
    partner = (d, (1 - zlo) * 16 + yx)
    up_ring = (((zhi + 1) % 4) * 2 + core, e)
    down_ring = (((zhi + 3) % 4) * 2 + core, e)
    z = zhi * 2 + zlo

    def column(k):
        other = (z + k) % 8
        return other, ((other // 2) * 2 + core, (other % 2) * 16 + yx)

    def plane(k):
        step = (k * 5) % 16
        return ((y + step // 4) % 4) * 4 + (x + step % 4) % 4

    def send(src, dst, s, r, target):
        pltpu.make_async_remote_copy(src, dst, s, r, target, MESH).start()

    def drain(ref, sem):
        pltpu.make_async_copy(ref, ref, sem).wait()

    bar = pltpu.get_barrier_semaphore()

    def greet(k, carry):
        pl.semaphore_signal(bar, inc=1, device_id=(d, (e + k) % 32), device_id_type=MESH)
        return carry

    lax.fori_loop(1, 32, greet, 0)
    pl.semaphore_signal(bar, inc=1, device_id=sibling, device_id_type=MESH)

    def greet_column(k, carry):
        pl.semaphore_signal(
            bar, inc=1, device_id=(((zhi + k) % 4) * 2 + core, e), device_id_type=MESH
        )
        pl.semaphore_signal(
            bar, inc=1, device_id=(((zhi + k) % 4) * 2 + core, (1 - zlo) * 16 + yx), device_id_type=MESH
        )
        return carry

    lax.fori_loop(1, 4, greet_column, 0)

    loads = [
        pltpu.make_async_copy(source, here, in_sem.at[i])
        for i, (source, here) in enumerate(
            (
                (ids_hbm, ids), (rw_hbm, rw), (tok_hbm, tok), (gate_hbm, gate),
                (up_hbm, up), (moe_hbm, moe), (w_hbm, w),
            )
        )
    ]
    for load in loads:
        load.start()
    load_ids, load_rw, load_tok, load_gate, load_up, load_moe, load_w = loads
    load_ids.wait()
    load_rw.wait()

    expert_row = lax.broadcasted_iota(jnp.int32, (EXPERTS, TOK), 0)
    token_lane = lax.broadcasted_iota(jnp.int32, (EXPERTS, TOK), 1)
    named = jnp.zeros((EXPERTS, TOK), F32)
    weights = jnp.zeros((EXPERTS, TOK), F32)
    for k in range(TOPK):
        match = ids[k : k + 1, :] == expert_row
        named = named + jnp.where(match, 1.0, 0.0)
        weights = weights + jnp.where(match, rw[k : k + 1, :], 0.0)
    weight_by_expert[...] = weights
    before = jnp.where(expert_row < token_lane, 1.0, 0.0).astype(BF)
    rank = dot(named.astype(BF), before)
    code = (named * (rank + 1.0)).astype(BF)
    flying_row = lax.broadcasted_iota(jnp.int32, (32, EXPERTS), 0)
    flying_lane = lax.broadcasted_iota(jnp.int32, (32, EXPERTS), 1)
    flying = jnp.where(flying_lane == EXP_DEV * flying_row, 1.0, 0.0).astype(BF)
    codes = dot(flying, code)
    flying_code[...] = codes
    flying_weight = dot(flying, weights.astype(BF)).astype(BF)
    meta[0, :16] = codes[:16].astype(BF)
    meta[0, 16:] = flying_weight[:16]
    meta[1, :16] = codes[16:].astype(BF)
    meta[1, 16:] = flying_weight[16:]

    half_row = lax.broadcasted_iota(jnp.int32, (HALF, 32), 0)
    half_lane = lax.broadcasted_iota(jnp.int32, (HALF, 32), 1)
    to_code = jnp.where(half_lane == half_row // MOST, 1.0, 0.0).astype(BF)
    to_weight = jnp.where(half_lane == 16 + half_row // MOST, 1.0, 0.0).astype(BF)
    place = (lax.broadcasted_iota(jnp.int32, (HALF, TOK), 0) % MOST + 1).astype(F32)

    def lay_out(half, about):
        placed = dot(to_code, about) == place
        placer[half] = jnp.where(placed, 1.0, 0.0).astype(BF)
        total = jnp.sum(jnp.where(placed, dot(to_weight, about), 0.0), 1, keepdims=True)
        w_send[half] = jnp.broadcast_to(total, (HALF, 128)).astype(BF)

    lay_out(0, meta[zlo])
    load_tok.wait()

    pl.semaphore_wait(bar, 38)

    send(meta.at[1 - zlo], meta_p, z_s, z_r.at[NC], partner)
    for c in range(NC):
        cols = pl.ds(c * DC, DC)
        send(tok.at[:, cols], tok_p.at[:, cols], z_s, z_r.at[c], partner)

    def pack(half, c):
        cols = pl.ds(c * DC, DC)
        chosen = placer[half]
        tokens = tok if half == 0 else tok_p
        for q in range(DC // 256):
            part = pl.ds(c * DC + q * 256, 256)
            snd[pl.ds(half * HALF, HALF), part] = dot(chosen, tokens[:, part]).astype(BF)
        source = zlo * 16 + yx if half == 0 else (1 - zlo) * 16 + yx
        recv[pl.ds(m16(source), 16), cols] = snd[pl.ds(m16(half * 16 + yx), 16), cols]

        def one(k, carry):
            target = plane(k)
            send(
                snd.at[pl.ds(m16(half * 16 + target), 16), cols],
                recv.at[pl.ds(m16(source), 16), cols],
                a_s, a_r.at[c, half], (d, zlo * 16 + target),
            )
            return carry

        lax.fori_loop(1, 16, one, 0)

    def give_weights(half):
        source = zlo * 16 + yx if half == 0 else (1 - zlo) * 16 + yx
        w_recv[pl.ds(m16(source), 16), :] = w_send[half, pl.ds(m16(yx), 16), :]

        def one(k, carry):
            target = plane(k)
            send(
                w_send.at[half, pl.ds(m16(target), 16)], w_recv.at[pl.ds(m16(source), 16)],
                w_s, w_r, (d, zlo * 16 + target),
            )
            return carry

        lax.fori_loop(1, 16, one, 0)

    def read_partner():
        drain(meta_p, z_r.at[NC])
        lay_out(1, meta_p[...])
        give_weights(1)

    def pack_partner(c):
        drain(tok_p.at[:, pl.ds(c * DC, DC)], z_r.at[c])
        pack(1, c)

    def gates(i, carry):
        part = pl.ds(pl.multiple_of(i * 32, 32), 32)
        g = gate[part, :].astype(F32)
        u = up[part, :].astype(F32)
        sigma = jax.nn.sigmoid(g)
        act = g * sigma
        active[part, :] = act
        gate_factor[part, :] = u * sigma * (1.0 + g * (1.0 - sigma))
        hidden[part, :] = (act * u).astype(BF)
        return carry

    def make_gates():
        load_gate.wait()
        load_up.wait()
        lax.fori_loop(0, SLOTS // 32, gates, 0)

    def turn(i, carry):
        part = pl.ds(pl.multiple_of(i * 512, 512), 512)
        moe_t[part, :] = moe[:, part].T
        return carry

    def turn_moe():
        load_moe.wait()
        lax.fori_loop(0, D // 512, turn, 0)

    def weigh(i, carry):
        part = pl.ds(pl.multiple_of(i * 128, 128), 128)
        scale = jnp.concatenate([w_recv[part, :].astype(F32)] * (FFE // 128), axis=1)
        hw_t[:, part] = (scale * hidden[part, :].astype(F32)).astype(BF).T
        return carry

    def weigh_hidden():
        drain(w_recv.at[pl.ds(0, SLOTS - 32)], w_r)
        lax.fori_loop(0, SLOTS // 128, weigh, 0)

    def arrive(c):
        for half in range(2):
            drain(recv.at[pl.ds(0, HALF - 16), pl.ds(c * DC, DC)], a_r.at[c, half])

    def make_term(c):
        arrive(c)
        for q in range(DC // 256):
            cols = pl.ds(c * DC + q * 256, 256)
            block = dot(hw_t[...], recv[:, cols]).astype(BF)
            term[:, :, :, cols] = block.reshape(4, 2, OWN, 256)
            send(term.at[:, 1 - core, :, cols], pair.at[:, :, cols], p_s, p_r.at[c], sibling)

    def make_hidden(c):
        if c == 1:
            load_w.wait()
        first = c - 1 if c < NC - 2 else c
        cols = pl.ds(first * DC, (c + 1 - first) * DC)

        def one(q, carry):
            part = pl.ds(pl.multiple_of(q * 256, 256), 256)
            block = dot(recv[:, cols], w[part, cols], 1, 1)
            if c == 1:
                hc[:, part] = block
            else:
                hc[:, part] = hc[:, part] + block
            return carry

        lax.fori_loop(0, FFE // 256, one, 0)

    def ways(c):
        return (
            (0, pl.ds(c * DC, DH), up_ring, 1),
            (1, pl.ds(c * DC + DH, DH), down_ring, -1),
        )

    def pair_sum(c):
        cols = pl.ds(c * DC, DC)
        drain(pair.at[:, :, cols], p_r.at[c])

        def add(block):
            both = term[block, core, :, cols].astype(F32) + pair[block, :, cols].astype(F32)
            psum[block, :, cols] = both.astype(BF)

        for way, part, target, sign in ways(c):
            block = (zhi + 4 - sign) % 4
            add(block)
            send(psum.at[block, :, part], ring.at[0, :, part], g_s, g_r.at[c, 0, way], target)
        add((zhi + 2) % 4)
        add(zhi)

    def ring_step(c, step):
        for way, part, target, sign in ways(c):
            drain(ring.at[step, :, part], g_r.at[c, step, way])
            block = (zhi + 8 - sign * (step + 2)) % 4
            total = ring[step, :, part].astype(F32) + psum[block, :, part].astype(F32)
            ring[step, :, part] = total.astype(BF)
            send(ring.at[step, :, part], ring.at[step + 1, :, part], g_s, g_r.at[c, step + 1, way], target)

    outs = [
        pltpu.make_async_copy(gate_v, gate_out, out_sem.at[0]),
        pltpu.make_async_copy(up_v, up_out, out_sem.at[1]),
        pltpu.make_async_copy(route_v, route_out, out_sem.at[2]),
        pltpu.make_async_copy(router_v, router_out, out_sem.at[3]),
    ]
    down_outs = [
        pltpu.make_async_copy(
            down_v.at[:, pl.ds(c * DC, DC)], down_out.at[:, pl.ds(c * DC, DC)], out_sem.at[4 + c]
        )
        for c in range(NC)
    ]

    def ring_end(c):
        for way, part, target, sign in ways(c):
            drain(ring.at[2, :, part], g_r.at[c, 2, way])
            down_v[:, part] = ring[2, :, part].astype(F32) + psum[zhi, :, part].astype(F32)
        down_outs[c].start()

    def dots(i, carry):
        part = pl.ds(pl.multiple_of(i * 128, 128), 128)
        total = jnp.zeros((128, 128), F32)
        for q in range(FFE // 128):
            cols = pl.ds(q * 128, 128)
            total = total + hidden[part, cols].astype(F32) * hc[part, cols]
        back_send[i] = jnp.sum(total.T, 0, keepdims=True)
        return carry

    def give_back(k, carry):
        target = (e + k) % 32
        send(back_send.at[target // 8], back_recv.at[e], b_s, b_r, (d, target))
        return carry

    def give_dots():
        lax.fori_loop(0, SLOTS // 128, dots, 0)
        back_recv[e] = back_send[e // 8]
        lax.fori_loop(1, 32, give_back, 0)

    def grads(i, carry):
        part = pl.ds(pl.multiple_of(i * 32, 32), 32)
        scale = jnp.concatenate([w_recv[part, :].astype(F32)] * (FFE // 128), axis=1)
        cot = hc[part, :] * scale
        up_v[part, :] = (cot * active[part, :]).astype(BF)
        gate_v[part, :] = (cot * gate_factor[part, :]).astype(BF)
        return carry

    def make_grads():
        lax.fori_loop(0, SLOTS // 32, grads, 0)
        outs[0].start()
        outs[1].start()

    def product(i):
        return dot(moe_t[pl.ds(pl.multiple_of(i * 512, 512), 512), :], logit[...], 1, 1)

    def product_sibling(k, carry):
        prod_b[k] = product(2 * k + 1 - core).astype(BF)
        send(prod_b.at[k], rp.at[k], rp_s, rp_r, sibling)
        return carry

    def product_own(k, carry):
        prod[k] = product(2 * k + core)
        return carry

    def router_terms():
        drain(back_recv.at[pl.ds(0, 31)], b_r)
        back = jnp.concatenate([back_recv[j] for j in range(32)], axis=0)
        back = pltpu.roll(back, (8 - e % 8) % 8 * 16, 1)
        flown = jnp.zeros((32, TOK), F32)
        for r in range(MOST):
            flown = flown + jnp.where(flying_code[...] == r + 1.0, back[:, r : r + 1], 0.0)
        stretch_row = lax.broadcasted_iota(jnp.int32, (EXPERTS, 32), 0)
        stretch_lane = lax.broadcasted_iota(jnp.int32, (EXPERTS, 32), 1)
        stretch = jnp.where(stretch_row == EXP_DEV * stretch_lane, 1.0, 0.0).astype(BF)
        high = flown.astype(BF)
        rest = flown - high.astype(F32)
        middle = rest.astype(BF)
        low = (rest - middle.astype(F32)).astype(BF)
        by_expert = dot(stretch, high) + dot(stretch, middle) + dot(stretch, low)
        for k in range(TOPK):
            picked = jnp.where(ids[k : k + 1, :] == expert_row, by_expert, 0.0)
            route_v[k : k + 1, :] = jnp.sum(picked, 0, keepdims=True)
        outs[2].start()
        mine = weight_by_expert[...]
        mixed = jnp.sum(mine * by_expert, 0, keepdims=True)
        logit[...] = (mine * (by_expert - mixed)).astype(BF)
        lax.fori_loop(0, 4, product_sibling, 0)
        lax.fori_loop(0, 4, product_own, 0)

    def pair_router(k, carry):
        both = prod[k] + rp[k].astype(F32)
        rq_send[pl.ds(2 * k, 2)] = both.astype(BF).reshape(2, HALF, 128)
        return carry

    def give_plane(k, carry):
        target = plane(k)
        send(rq_send.at[:, pl.ds(m16(target), 16)], rq.at[yx], rq_s, rq_r, (d, zlo * 16 + target))
        return carry

    def router_pair():
        drain(rp, rp_r)
        lax.fori_loop(0, 4, pair_router, 0)
        rq[yx] = rq_send[:, pl.ds(m16(yx), 16), :]
        lax.fori_loop(1, 16, give_plane, 0)

    def add_plane(k, total):
        return total + rq[k].astype(F32)

    def give_column(k, carry):
        other, target = column(k)
        send(rz_send.at[other], rz.at[z], rz_s, rz_r, target)
        return carry

    def router_plane():
        drain(rq.at[pl.ds(0, 15)], rq_r)
        rz_send[...] = lax.fori_loop(1, 16, add_plane, rq[0].astype(F32)).astype(BF)
        rz[z] = rz_send[z]
        lax.fori_loop(1, 8, give_column, 0)

    def router_end():
        drain(rz.at[pl.ds(0, 7)], rz_r)
        total = rz[0].astype(F32)
        for k in range(1, 8):
            total = total + rz[k].astype(F32)
        router_v[...] = 0.015625 * total
        outs[3].start()

    pack(0, 0)
    pack(0, 1)
    give_weights(0)
    make_gates()
    read_partner()
    turn_moe()
    pack_partner(0)
    pack(0, 2)
    weigh_hidden()
    pack_partner(1)
    pack(0, 3)
    pack_partner(2)
    pack(0, 4)
    make_term(0)
    pack_partner(3)
    pack(0, 5)
    pair_sum(0)
    pack_partner(4)
    pack(0, 6)
    make_term(1)
    make_hidden(1)
    pack_partner(5)
    pack(0, 7)
    pack_partner(6)
    make_term(2)
    pair_sum(1)
    pack_partner(7)
    pair_sum(2)
    ring_step(0, 0)
    make_term(3)
    make_hidden(3)
    ring_step(1, 0)
    ring_step(2, 0)
    pair_sum(3)
    ring_step(0, 1)
    make_term(4)
    ring_step(1, 1)
    ring_step(2, 1)
    pair_sum(4)
    make_term(5)
    make_hidden(5)
    ring_step(3, 0)
    pair_sum(5)
    ring_end(0)
    make_term(6)
    make_hidden(6)
    ring_end(1)
    make_term(7)
    make_hidden(7)
    give_dots()
    pair_sum(6)
    ring_step(3, 1)
    ring_step(4, 0)
    pair_sum(7)
    ring_step(5, 0)
    ring_end(2)
    make_grads()
    router_terms()
    ring_step(6, 0)
    ring_step(4, 1)
    router_pair()
    ring_end(3)
    ring_step(7, 0)
    ring_step(5, 1)
    ring_step(6, 1)
    router_plane()
    ring_step(7, 1)
    ring_end(4)
    router_end()
    ring_end(5)
    ring_end(6)
    ring_end(7)

    drain(meta_p, z_s)
    drain(tok_p, z_s)
    drain(w_recv.at[pl.ds(0, SLOTS - 32)], w_s)
    drain(recv.at[pl.ds(0, SLOTS - 32)], a_s)
    drain(pair, p_s)
    drain(ring, g_s)
    drain(back_recv.at[pl.ds(0, 31)], b_s)
    drain(rp, rp_s)
    drain(rq.at[pl.ds(0, 15)], rq_s)
    drain(rz.at[pl.ds(0, 7)], rz_s)
    for copy in outs + down_outs:
        copy.wait()


def per_device(out_cot, route_ids, route_weight, saved_gate, saved_up, down_weight, moe_input):
    anywhere = pl.BlockSpec(memory_space=pl.ANY)
    dma = pltpu.SemaphoreType.DMA
    scratch = [
        ((TOK, D), BF),
        ((TOPK, TOK), jnp.int32),
        ((TOPK, TOK), F32),
        ((SLOTS, FFE), BF),
        ((SLOTS, FFE), BF),
        ((FFE, D), BF),
        ((TOK, D), BF),
        ((D, TOK), BF),
        ((2, HALF, TOK), BF),
        ((2, 32, TOK), BF),
        ((32, TOK), BF),
        ((32, TOK), F32),
        ((TOK, D), BF),
        ((EXPERTS, TOK), F32),
        ((2, HALF, 128), BF),
        ((SLOTS, 128), BF),
        ((SLOTS, D), BF),
        ((SLOTS, D), BF),
        ((SLOTS, FFE), BF),
        ((SLOTS, FFE), F32),
        ((SLOTS, FFE), F32),
        ((FFE, SLOTS), BF),
        ((SLOTS, FFE), F32),
        ((4, 2, OWN, D), BF),
        ((4, OWN, D), BF),
        ((4, OWN, D), BF),
        ((3, OWN, D), BF),
        ((4, 1, 128), F32),
        ((32, 1, 128), F32),
        ((4, 512, 128), F32),
        ((4, 512, 128), BF),
        ((4, 512, 128), BF),
        ((8, HALF, 128), BF),
        ((16, 8, 16, 128), BF),
        ((8, 16, 128), BF),
        ((8, 16, 128), BF),
        ((SLOTS, FFE), BF),
        ((SLOTS, FFE), BF),
        ((OWN, D), F32),
        ((TOPK, TOK), F32),
        ((16, EXPERTS), F32),
    ]
    sems = [
        dma((7,)), dma(()), dma((NC + 1,)), dma(()), dma(()), dma(()), dma((NC, 2)),
        dma(()), dma((NC,)), dma(()), dma((NC, 3, 2)), dma(()), dma(()),
        dma(()), dma(()), dma(()), dma(()), dma(()), dma(()), dma((4 + NC,)),
        pltpu.VMEM((EXPERTS, TOK), BF),
    ]
    outs = pl.pallas_call(
        body,
        out_shape=(
            jax.ShapeDtypeStruct((SLOTS, FFE), BF),
            jax.ShapeDtypeStruct((SLOTS, FFE), BF),
            jax.ShapeDtypeStruct((OWN, D), F32),
            jax.ShapeDtypeStruct((TOPK, TOK), F32),
            jax.ShapeDtypeStruct((16, EXPERTS), F32),
        ),
        in_specs=[anywhere] * 7,
        out_specs=(anywhere,) * 5,
        scratch_shapes=[pltpu.VMEM(shape, kind) for shape, kind in scratch] + sems,
        compiler_params=pltpu.CompilerParams(
            collective_id=0, has_side_effects=True, vmem_limit_bytes=58 * 2**20
        ),
    )(
        out_cot, route_ids.T, route_weight.T, saved_gate[0, 0], saved_up[0, 0],
        down_weight[0], moe_input,
    )
    gate_grad, up_grad, down_grad, route_grad, router_grad = hand_over(outs)
    return gate_grad[None, None], up_grad[None, None], down_grad[None], route_grad.T, router_grad


def hand_over_body(*refs):
    sources, targets, held, load_sem, store_sem = refs[:5], refs[5:10], refs[10:15], refs[15], refs[16]
    loads, stores = [], []
    for source, target, here in zip(sources, targets, held):
        pieces = 4 if source.shape[0] >= 64 else 1
        rows = source.shape[0] // pieces
        for i in range(pieces):
            part, n = pl.ds(i * rows, rows), len(loads)
            loads.append(pltpu.make_async_copy(source.at[part], here.at[part], load_sem.at[n]))
            stores.append(pltpu.make_async_copy(here.at[part], target.at[part], store_sem.at[n]))
    for load in loads:
        load.start()
    for load, store in zip(loads, stores):
        load.wait()
        store.start()
    for store in stores:
        store.wait()


def hand_over(arrays):
    anywhere = pl.BlockSpec(memory_space=pl.ANY)
    return pl.pallas_call(
        hand_over_body,
        out_shape=[jax.ShapeDtypeStruct(a.shape, a.dtype) for a in arrays],
        in_specs=[anywhere] * 5,
        out_specs=[anywhere] * 5,
        scratch_shapes=[pltpu.VMEM(a.shape, a.dtype) for a in arrays]
        + [pltpu.SemaphoreType.DMA((14,))] * 2,
        compiler_params=pltpu.CompilerParams(vmem_limit_bytes=58 * 2**20),
    )(*arrays)


def solution(mesh):
    placed = (
        P(("dp", "expert"), None),
        P(("dp", "expert"), None),
        P(("dp", "expert"), None),
        P("dp", "expert", None, None),
        P("dp", "expert", None, None),
        P("expert", None, None),
        P(("dp", "expert"), None),
    )
    return jax.shard_map(
        per_device,
        mesh=mesh,
        in_specs=placed,
        out_specs=(
            P("dp", "expert", None, None),
            P("dp", "expert", None, None),
            P("expert", "dp", None),
            P(("dp", "expert"), None),
            P(("dp", "expert"), None),
        ),
        check_vma=False,
    )
```
